256 devices in a mesh: dp: 64 (over x, z, core), mp: 4 (over y).
Axes of the slice: x: 4, y: 4, z: 8, core: 2. Of those that a mesh axis runs over, the one named last changes fastest.
Arguments:
- inputs: bfloat16 [64, 512, 4096], P('dp'), may hold values from -16 to 16
- w_query: bfloat16 [4096, 2048], P(None, 'mp'), may hold values from -0.09375 to 0.09375
- cache_kv: bfloat16 [512, 2, 128, 2048], P('dp', None, None, 'mp'), may hold values from -240 to 240
- nb_owner: int32 [64, 8, 2], P('dp'), may hold values from 0 to 63, as said below
- nb_row: int32 [64, 8, 2], P('dp'), may hold values from 0 to 7
- out_grad: bfloat16 [64, 512, 2048], P('dp', None, 'mp'), may hold values from -6 to 6
Outputs:
- attended: bfloat16 [64, 512, 2048], P('dp', None, 'mp')
- input_grad: bfloat16 [64, 512, 4096], P('dp', None, 'mp')
- query_grad: float32 [4096, 2048], P('dp', 'mp')
The draws below stay inside these ranges and needn't reach their ends.
Inputs may be any that keep to these rules, and one draw needn't show every extreme that they name: `nb_owner`: within one sequence no owner is named more than 1 times; one owner, the same for every sequence, is named exactly 1 times by each sequence.
All inputs are finite; a program needn't handle non-finite values.
Results may differ from the reference program's by a relative error of at most 0.02.
The reference program's roundings to bfloat16 on the way (of `queries`, `probs_bf`, `dscore` and `dquery`) count: a program that leaves them out, or rounds other values in their place, can miss the bound.
Values may be sent and summed in bfloat16 or wider, within the bound.
No kernel may reach another device: no remote copies, remote signals or barrier semaphores. Data moves between devices by JAX's collectives and lax.ppermute only.
A program may use at most 128 MiB of HBM per device.

```python
import jax
import jax.numpy as jnp
from jax import lax

D = 4096
HEADS = 16
HEAD_DIM = 128
STRETCH = 64
NB_LEN = 128
NEIGH = 2
LEN = 512
DB_ROWS = 8
SEQS = 64
STRETCHES = 8
REQS = 16
CAP = 1
ATT_WIDTH = 2048
N_DP = 64
N_MP = 4


def draw_nb_owner(key, part):
    key = jax.random.fold_in(key, 11)
    hot_key, seq_key = jax.random.split(key)
    hot_owner = jax.random.randint(hot_key, (), 0, N_DP)
    labels = jnp.arange(N_DP * CAP, dtype=jnp.int32)

    def one_seq(seq_number):
        seq_fold = jax.random.fold_in(seq_key, seq_number)
        first_key, second_key = jax.random.split(seq_fold)
        shuffled = jax.random.permutation(first_key, N_DP * CAP).astype(jnp.int32)
        priority = jnp.where(labels // CAP == hot_owner, shuffled - N_DP * CAP, shuffled)
        chosen = jnp.argsort(priority, stable=True)[:REQS].astype(jnp.int32)
        owner_list = chosen // CAP
        placed = jax.random.permutation(second_key, owner_list)
        return placed.reshape(STRETCHES, NEIGH).astype(jnp.int32)
    return jax.vmap(one_seq)(jnp.arange(SEQS, dtype=jnp.int32))


def draw_cache_kv(key, part):
    key = jax.random.fold_in(key, 23)
    shape = (N_DP * DB_ROWS, 2, NB_LEN, ATT_WIDTH)
    base = jax.random.truncated_normal(key, -6.0, 6.0, shape, jnp.float32)
    return base.astype(jnp.bfloat16)


def plant(drawn, stream_key, least, top_value):
    spot = [jax.random.randint(jax.random.fold_in(stream_key, axis), (), 0, length) for axis, length in enumerate(drawn.shape)]
    longest = drawn.shape.index(max(drawn.shape))
    next_to = spot[:longest] + [(spot[longest] + 1) % drawn.shape[longest]] + spot[longest + 1:]
    return drawn.at[tuple(spot)].set(least).at[tuple(next_to)].set(top_value)


def spiked(entries, stream_key, source, target, blocks, factor):
    owner, partner = [(jnp.arange(entries.shape[axis_at]) // (entries.shape[axis_at] // blocks)).reshape([-1 if axis == axis_at else 1 for axis in range(entries.ndim)]) for axis_at in (source, target)]
    chosen = jax.random.permutation(stream_key, blocks)[partner]
    strong = (owner == chosen) | (owner == (partner + blocks // 2) % blocks)
    return jnp.where(strong, factor * entries, entries)


def levels(own_key, shape, pieces, least, largest):
    gain, own = 1.0, jax.random.fold_in(own_key, 6)
    for dim, blocks in pieces:
        heights = jnp.exp(jax.random.uniform(jax.random.fold_in(own, dim), (blocks,), jnp.float32, least / len(pieces), largest / len(pieces)))
        gain = gain * jnp.repeat(heights, shape[dim] // blocks).reshape([-1 if axis == dim else 1 for axis in range(len(shape))])
    return gain


def bell_draw(own_key, dims, scale, bound, pieces=(), held_as=jnp.bfloat16):
    drawn = scale * jax.random.normal(own_key, dims, jnp.float32)
    if pieces:
        drawn = drawn * levels(own_key, dims, pieces, -0.22, 0.18)
    return jnp.clip(drawn, -bound, bound).astype(held_as)


def heavy_noise(rng, shape, deviation, bound, shards, heavy, held_as=jnp.bfloat16):
    drawn = deviation * jax.random.normal(rng, shape, jnp.float32)
    if shards:
        drawn = drawn * levels(rng, shape, shards, -0.22, 0.18)
    return jnp.clip(spiked(drawn, jax.random.fold_in(rng, 3), *heavy), -bound, bound).astype(held_as)


def setup_inputs(seed: int = 0) -> dict:
    key_of = jax.random.split(jax.random.key(seed), 7)
    inputs = heavy_noise(key_of[0], (SEQS, LEN, D), 1.0, 16.0, ((0, 64),), (0, 2, 64, 4.0))
    w_query = bell_draw(key_of[1], (D, ATT_WIDTH), D ** -0.5, 0.09375, ((1, 4),))
    cache_kv = draw_cache_kv(jax.random.fold_in(key_of[6], 71), 0)
    nb_owner = draw_nb_owner(jax.random.fold_in(key_of[6], 71), 0)
    nb_row = plant(jax.random.randint(key_of[4], (SEQS, STRETCHES, NEIGH), 0, DB_ROWS), jax.random.fold_in(key_of[4], 1), 0, DB_ROWS - 1).astype(jnp.int32)
    out_grad = bell_draw(key_of[5], (SEQS, LEN, ATT_WIDTH), 1.0, 6.0, ((0, 64), (2, 4)))
    return {"inputs": inputs, "w_query": w_query, "cache_kv": cache_kv, "nb_owner": nb_owner, "nb_row": nb_row, "out_grad": out_grad}


def stretch_attention(queries, seq_grad, keys, values):
    lead_rows = STRETCH - 1
    local_heads = keys.shape[2]
    score_scale = HEAD_DIM ** -0.5

    def shifted(array):
        tail = jnp.zeros((lead_rows, array.shape[1]), array.dtype)
        return jnp.concatenate([array[lead_rows:], tail], 0).reshape(-1, STRETCH, local_heads, HEAD_DIM)

    def unshift(array):
        flat = array.reshape(-1, local_heads * HEAD_DIM)
        head = jnp.zeros((lead_rows, flat.shape[1]), flat.dtype)
        return jnp.concatenate([head, flat[:flat.shape[0] - lead_rows]], 0)

    q_blocks = shifted(queries).astype(jnp.float32)
    g_blocks = shifted(seq_grad).astype(jnp.float32)
    key_f = keys.astype(jnp.float32)
    value_f = values.astype(jnp.float32)
    scores = jnp.einsum('cqhd,ckhd->chqk', q_blocks, key_f) * score_scale
    row_max = jnp.max(scores, axis=-1, keepdims=True)
    exp_scores = jnp.exp(scores - row_max)
    probs = exp_scores / jnp.sum(exp_scores, axis=-1, keepdims=True)
    probs_bf = probs.astype(jnp.bfloat16)
    outputs = jnp.einsum('chqk,ckhd->cqhd', probs_bf.astype(jnp.float32), value_f)
    dprob = jnp.einsum('cqhd,ckhd->chqk', g_blocks, value_f)
    delta = jnp.sum(dprob * probs, axis=-1, keepdims=True)
    dscore = (probs * (dprob - delta) * score_scale).astype(jnp.bfloat16)
    dquery = jnp.einsum('chqk,ckhd->cqhd', dscore.astype(jnp.float32), key_f)
    return unshift(outputs).astype(jnp.bfloat16), unshift(dquery).astype(jnp.bfloat16)


def reference(inputs, w_query, cache_kv, nb_owner, nb_row, out_grad):
    group_width = ATT_WIDTH // N_MP

    def per_seq(running, slices):
        seq_tokens, seq_owner, seq_rows, seq_grad = slices
        queries = jnp.dot(seq_tokens, w_query, preferred_element_type=jnp.float32).astype(jnp.bfloat16)
        flat_index = (seq_owner * DB_ROWS + seq_rows).reshape(-1).astype(jnp.int32)
        gathered = cache_kv[flat_index].reshape(STRETCHES, NEIGH, 2, NB_LEN, HEADS, HEAD_DIM)
        keys = gathered[:, :, 0].reshape(STRETCHES, NEIGH * NB_LEN, HEADS, HEAD_DIM)
        values = gathered[:, :, 1].reshape(STRETCHES, NEIGH * NB_LEN, HEADS, HEAD_DIM)
        attended, dquery = stretch_attention(queries, seq_grad, keys, values)
        input_grad = jnp.zeros((LEN, D), jnp.float32)
        for member in range(N_MP):
            lower = member * group_width
            upper = lower + group_width
            partial_value = jnp.dot(dquery[:, lower:upper], w_query[:, lower:upper].T, preferred_element_type=jnp.float32)
            rounded = lax.optimization_barrier(partial_value.astype(jnp.bfloat16))
            input_grad = input_grad + rounded.astype(jnp.float32)
        running = running + jnp.dot(seq_tokens.T, dquery, preferred_element_type=jnp.float32)
        return running, (attended, input_grad.astype(jnp.bfloat16))

    start_grad = jnp.zeros((D, ATT_WIDTH), jnp.float32)
    query_grad, (attended, input_grad) = lax.scan(per_seq, start_grad, (inputs, nb_owner, nb_row, out_grad))
    return attended, input_grad, query_grad
```

```python
import functools

import jax
import jax.numpy as jnp
from jax import lax
from jax.experimental import pallas as pl
from jax.experimental.pallas import tpu as pltpu
from jax.sharding import Mesh
from jax.sharding import PartitionSpec as P

HEAD_DIM = 128
STRETCH = 64
LEAD = STRETCH - 1
TILE = 16
PLANE = ("x", "core")
DP = ("x", "z", "core")
CHUNKS = ((0, 3), (3, 6), (6, 8))
BF16, F32 = jnp.bfloat16, jnp.float32


def pick_kernel(ids_ref, tiles_ref, out_ref, *, slots):
    seq = pl.program_id(0)

    for slot in range(slots):
        out_ref[0, slot] = tiles_ref[ids_ref[seq * slots + slot]]


def pick(ids, tiles):
    seqs, slots = ids.shape
    return pl.pallas_call(
        functools.partial(pick_kernel, slots=slots),
        grid_spec=pltpu.PrefetchScalarGridSpec(
            num_scalar_prefetch=1,
            grid=(seqs,),
            in_specs=[pl.BlockSpec(tiles.shape, lambda s, ids: (0, 0, 0))],
            out_specs=pl.BlockSpec((1, slots) + tiles.shape[1:], lambda s, ids: (s, 0, 0, 0)),
        ),
        out_shape=jax.ShapeDtypeStruct((seqs, slots) + tiles.shape[1:], tiles.dtype),
        compiler_params=pltpu.CompilerParams(vmem_limit_bytes=32 << 20),
        cost_estimate=pl.CostEstimate(flops=0, bytes_accessed=6 << 20, transcendentals=0),
        name="pick",
    )(ids.reshape(-1), tiles)


def attend_kernel(q_ref, g_ref, kv_ref, out_ref, dq_ref, *, heads):
    scale = HEAD_DIM ** (-0.5)
    both = (((1,), (1,)), ((), ()))
    for head in range(heads):
        cols = slice(head * HEAD_DIM, (head + 1) * HEAD_DIM)
        keys = kv_ref[0, head].reshape(-1, HEAD_DIM)
        values = kv_ref[1, head].reshape(-1, HEAD_DIM)
        scores = lax.dot_general(q_ref[:, cols], keys, both, preferred_element_type=F32) * scale
        exps = jnp.exp(scores - jnp.max(scores, axis=-1, keepdims=True))
        probs = exps / jnp.sum(exps, axis=-1, keepdims=True)
        out_ref[:, cols] = jnp.dot(
            probs.astype(BF16), values, preferred_element_type=F32
        ).astype(BF16)
        dprob = lax.dot_general(g_ref[:, cols], values, both, preferred_element_type=F32)
        delta = jnp.sum(dprob * probs, axis=-1, keepdims=True)
        dscore = (probs * (dprob - delta) * scale).astype(BF16)
        dq_ref[:, cols] = jnp.dot(dscore, keys, preferred_element_type=F32).astype(BF16)


def attend(q, g, kv, neigh):
    rows, width = q.shape
    count = rows // STRETCH
    _, heads, tiles, slots, _, _ = kv.shape
    block = pl.BlockSpec((STRETCH, width), lambda c: (c, 0))
    return pl.pallas_call(
        functools.partial(attend_kernel, heads=heads),
        grid=(count,),
        in_specs=[
            block,
            block,
            pl.BlockSpec((2, heads, tiles, neigh, TILE, HEAD_DIM), lambda c: (0, 0, 0, c, 0, 0)),
        ],
        out_specs=[block, block],
        out_shape=[jax.ShapeDtypeStruct(q.shape, BF16)] * 2,
        compiler_params=pltpu.CompilerParams(vmem_limit_bytes=32 << 20),
        cost_estimate=pl.CostEstimate(
            flops=10 * rows * width * neigh * tiles * TILE, bytes_accessed=kv.size * 2, transcendentals=0
        ),
        name="attend",
    )(q, g, kv)


def local(inputs, w_query, cache_kv, nb_owner, nb_row, out_grad):
    nx, nz, nc = (lax.axis_size(a) for a in DP)
    ndp = nx * nz * nc
    tokens, grad_rows = inputs[0], out_grad[0]
    length, d = tokens.shape
    width = w_query.shape[1]
    heads = width // HEAD_DIM
    db_rows, _, nb_len, _ = cache_kv.shape
    _, stretches, neigh = nb_owner.shape
    tiles = nb_len // TILE

    own_ids = (nb_owner * db_rows + nb_row).reshape(-1)
    ids = lax.all_gather(own_ids, DP, tiled=False)

    cut = cache_kv.reshape(db_rows, 2, tiles, TILE, heads, HEAD_DIM)
    cut = cut.transpose(1, 4, 2, 0, 3, 5).reshape(ndp, db_rows, TILE, HEAD_DIM)
    held = lax.all_to_all(cut, DP, split_axis=0, concat_axis=0, tiled=True)
    held = held.reshape(ndp * db_rows, TILE, HEAD_DIM)

    def shifted(array):
        return jnp.concatenate([array[LEAD:], jnp.zeros((LEAD, array.shape[1]), array.dtype)], 0)

    moved = shifted(tokens)
    q = jnp.dot(moved, w_query, preferred_element_type=F32).astype(BF16)
    g = shifted(grad_rows)

    share = moved.reshape(length, nx, nz, nc, -1).transpose(1, 3, 0, 2, 4).reshape(nx * nc, length, -1)
    share = lax.all_to_all(share, PLANE, split_axis=0, concat_axis=0, tiled=True)

    outs, grads, total = [], [], 0.0
    for first, last in CHUNKS:
        lo, hi = first * STRETCH, last * STRETCH
        slots = slice(first * neigh, last * neigh)
        send = pick(ids[:, slots], held)
        got = lax.all_to_all(send, DP, split_axis=0, concat_axis=0, tiled=True)
        got = got.reshape(2, heads, tiles, (last - first) * neigh, TILE, HEAD_DIM)
        out, dq = attend(q[lo:hi], g[lo:hi], got, neigh)
        rows = min(hi, length - LEAD) - lo
        keep = -(-rows // TILE) * TILE
        dq = jnp.where(jnp.arange(keep)[:, None] < rows, dq[:keep], 0)
        outs.append(out[:rows])
        part = lax.dot_general(
            dq, w_query, (((1,), (1,)), ((), ())), preferred_element_type=F32
        ).astype(BF16)
        part = part.reshape(keep, lax.axis_size("mp"), -1).transpose(1, 0, 2)
        part = lax.all_to_all(part, "mp", split_axis=0, concat_axis=0, tiled=True)
        part = jnp.sum(part.astype(F32), axis=0).astype(BF16)
        grads.append(part[:rows])
        plane_dq = lax.all_gather(dq, PLANE, tiled=False)
        total += jnp.einsum("std,stf->df", share[:, lo : lo + keep], plane_dq, preferred_element_type=F32)

    query_grad = lax.psum_scatter(total, "z", scatter_dimension=0, tiled=True)
    attended = jnp.concatenate([jnp.zeros((LEAD, width), BF16)] + outs, 0)
    input_grad = jnp.concatenate([jnp.zeros((LEAD, d // lax.axis_size("mp")), BF16)] + grads, 0)
    return attended[None], input_grad[None], query_grad


def solution(mesh):
    fine = Mesh(mesh.devices.reshape(4, 8, 2, 4), ("x", "z", "core", "mp"))
    return jax.shard_map(
        local,
        mesh=fine,
        in_specs=(
            P(DP, None, None),
            P(None, "mp"),
            P(DP, None, None, "mp"),
            P(DP, None, None),
            P(DP, None, None),
            P(DP, None, "mp"),
        ),
        out_specs=(P(DP, None, "mp"), P(DP, None, "mp"), P(DP, "mp")),
        check_vma=False,
    )
```

```python
import functools

import jax
import jax.numpy as jnp
from jax import lax
from jax.experimental import pallas as pl
from jax.experimental.pallas import tpu as pltpu
from jax.sharding import Mesh
from jax.sharding import PartitionSpec as P

HEAD_DIM = 128
STRETCH = 64
LEAD = STRETCH - 1
TILE = 16
SKIP = LEAD // TILE * TILE
DP = ("x", "z", "core")
VMEM = 56 << 20
BF16, F32 = jnp.bfloat16, jnp.float32
BOTH_LAST = (((1,), (1,)), ((), ()))
BOTH_FIRST = (((0,), (0,)), ((), ()))


def cut_kernel(owner_ref, row_ref, cache_ref, out_ref):
    rows = cache_ref.shape[0]
    stretches, neigh = owner_ref.shape
    lane = lax.broadcasted_iota(jnp.int32, (TILE, HEAD_DIM), 1)
    named = jnp.zeros((TILE, HEAD_DIM), F32)
    for s in range(stretches):
        for n in range(neigh):
            at = s * neigh + n
            named = jnp.where(lane == at, owner_ref[s, n].astype(F32), named)
            named = jnp.where(lane == at + stretches * neigh, row_ref[s, n].astype(F32), named)
    for tile in range(out_ref.shape[0]):
        out_ref[tile, :rows] = cache_ref[:, 0, tile * TILE : (tile + 1) * TILE]
        out_ref[tile, rows] = named.astype(BF16)


def cut(nb_owner, nb_row, cache):
    rows, _, nb_len, width = cache.shape
    tiles, heads = nb_len // TILE, width // HEAD_DIM
    return pl.pallas_call(
        cut_kernel,
        grid=(2, heads),
        in_specs=[
            pl.BlockSpec(memory_space=pltpu.SMEM),
            pl.BlockSpec(memory_space=pltpu.SMEM),
            pl.BlockSpec((rows, 1, nb_len, HEAD_DIM), lambda a, h: (0, a, 0, h)),
        ],
        out_specs=pl.BlockSpec((tiles, rows + 1, TILE, HEAD_DIM), lambda a, h: (a * heads + h, 0, 0, 0)),
        out_shape=jax.ShapeDtypeStruct((2 * heads * tiles, rows + 1, TILE, HEAD_DIM), BF16),
        compiler_params=pltpu.CompilerParams(vmem_limit_bytes=VMEM),
        cost_estimate=pl.CostEstimate(flops=0, bytes_accessed=4 << 20, transcendentals=0),
        name="cut",
    )(nb_owner, nb_row, cache)


def pick_kernel(ids_ref, tiles_ref, out_ref, *, slots):
    base = pl.program_id(0) * slots
    for slot in range(slots):
        out_ref[slot] = tiles_ref[ids_ref[base + slot]]


def pick(ids, tiles):
    count, slots = ids.shape[0], 64
    return pl.pallas_call(
        functools.partial(pick_kernel, slots=slots),
        grid_spec=pltpu.PrefetchScalarGridSpec(
            num_scalar_prefetch=1,
            grid=(count // slots,),
            in_specs=[pl.BlockSpec(tiles.shape, lambda s, ids: (0, 0, 0))],
            out_specs=pl.BlockSpec((slots,) + tiles.shape[1:], lambda s, ids: (s, 0, 0)),
        ),
        out_shape=jax.ShapeDtypeStruct((count,) + tiles.shape[1:], tiles.dtype),
        compiler_params=pltpu.CompilerParams(vmem_limit_bytes=VMEM),
        cost_estimate=pl.CostEstimate(flops=0, bytes_accessed=6 << 20, transcendentals=0),
        name="pick",
    )(ids, tiles)


def attend_kernel(q_ref, g_ref, kv_ref, out_ref, dq_ref, *, heads):
    scale = HEAD_DIM ** (-0.5)
    cols = [slice(h * HEAD_DIM, (h + 1) * HEAD_DIM) for h in range(heads)]
    keys = [kv_ref[0, h].reshape(-1, HEAD_DIM) for h in range(heads)]
    values = [kv_ref[1, h].reshape(-1, HEAD_DIM) for h in range(heads)]
    scores = [
        lax.dot_general(q_ref[:, c], k, BOTH_LAST, preferred_element_type=F32)
        for c, k in zip(cols, keys)
    ]
    dprobs = [
        lax.dot_general(g_ref[:, c], v, BOTH_LAST, preferred_element_type=F32)
        for c, v in zip(cols, values)
    ]
    probs, dscores = [], []
    for score, dprob in zip(scores, dprobs):
        score = score * scale
        exps = jnp.exp(score - jnp.max(score, axis=-1, keepdims=True))
        prob = exps * (1.0 / jnp.sum(exps, axis=-1, keepdims=True))
        delta = jnp.sum(dprob * prob, axis=-1, keepdims=True)
        probs.append(prob.astype(BF16))
        dscores.append((prob * (dprob - delta) * scale).astype(BF16))
    for c, k, v, prob, dscore in zip(cols, keys, values, probs, dscores):
        out_ref[:, c] = jnp.dot(prob, v, preferred_element_type=F32).astype(BF16)
        dq_ref[:, c] = jnp.dot(dscore, k, preferred_element_type=F32).astype(BF16)


def attend(q, g, kv, neigh):
    rows, width = q.shape
    count = rows // STRETCH
    _, heads, tiles, slots, _, _ = kv.shape
    block = pl.BlockSpec((STRETCH, width), lambda c: (c, 0))
    return pl.pallas_call(
        functools.partial(attend_kernel, heads=heads),
        grid=(count,),
        in_specs=[
            block,
            block,
            pl.BlockSpec((2, heads, tiles, neigh, TILE, HEAD_DIM), lambda c: (0, 0, 0, c, 0, 0)),
        ],
        out_specs=[block, block],
        out_shape=[jax.ShapeDtypeStruct(q.shape, BF16)] * 2,
        compiler_params=pltpu.CompilerParams(vmem_limit_bytes=VMEM),
        cost_estimate=pl.CostEstimate(
            flops=10 * rows * width * neigh * tiles * TILE, bytes_accessed=kv.size * 2, transcendentals=0
        ),
        name="attend",
    )(q, g, kv)


def step(array, axis, by):
    size = lax.axis_size(axis)
    return lax.ppermute(array, axis, [(i, (i + by) % size) for i in range(size)])


def local(inputs, w_query, cache_kv, nb_owner, nb_row, out_grad):
    nx, nz, nc = (lax.axis_size(a) for a in DP)
    ndp, nmp = nx * nz * nc, lax.axis_size("mp")
    mx, mz, mc = (lax.axis_index(a) for a in DP)
    my = lax.axis_index("mp")
    tokens, grad_rows = inputs[0], out_grad[0]
    length, d = tokens.shape
    width = w_query.shape[1]
    heads = width // HEAD_DIM
    db_rows, _, nb_len, _ = cache_kv.shape
    _, stretches, neigh = nb_owner.shape
    requests = stretches * neigh
    tiles = nb_len // TILE
    real = length - LEAD

    message = cut(nb_owner[0], nb_row[0], cache_kv)
    held = lax.all_to_all(message, DP, split_axis=0, concat_axis=0, tiled=True)
    named = held[:, db_rows, 0, : 2 * requests].astype(jnp.int32)
    ids = named[:, :requests] * (db_rows + 1) + named[:, requests:]
    send = pick(ids.reshape(-1), held.reshape(-1, TILE, HEAD_DIM))
    got = lax.all_to_all(
        send.reshape(ndp, requests, TILE, HEAD_DIM), DP, split_axis=0, concat_axis=0, tiled=True
    )

    def shifted(array):
        return jnp.concatenate([array[LEAD:], jnp.zeros((LEAD, array.shape[1]), array.dtype)], 0)

    q = shifted(jnp.dot(tokens, w_query, preferred_element_type=F32).astype(BF16))
    g = shifted(grad_rows)

    late, weights, _ = lax.optimization_barrier((tokens, w_query, held))
    block = d // nx
    share = [lax.dynamic_slice(late, (SKIP, (mx + by) % nx * block), (length - SKIP, block)) for by in range(nx)]
    share = [step(a, "x", by) if by else a for by, a in enumerate(share)]
    block = d // nmp
    fans = [lax.dynamic_slice(weights, ((my + by) % nmp * block, 0), (block, width)) for by in range(nmp)]
    fans = [step(a, "mp", by) if by else a for by, a in enumerate(fans)]

    out, dq = attend(q, g, got.reshape(2, heads, tiles, requests, TILE, HEAD_DIM), neigh)
    dq = jnp.concatenate([jnp.zeros((LEAD - SKIP, width), BF16), dq[:real]], 0)

    total = 0.0
    for by in range(nx):
        near = step(dq, "x", by) if by else dq
        total += lax.dot_general(share[by], near, BOTH_FIRST, preferred_element_type=F32)
    total = total.reshape(nz, nc, -1, width)
    mine = lax.dynamic_index_in_dim(total, mc, 1, keepdims=False)
    mine += step(lax.dynamic_index_in_dim(total, 1 - mc, 1, keepdims=False), "core", 1)
    query_grad = lax.dynamic_index_in_dim(mine, mz, 0, keepdims=False)
    for by in range(1, nz):
        query_grad += step(lax.dynamic_index_in_dim(mine, (mz + by) % nz, 0, keepdims=False), "z", by)

    part = 0.0
    for by in range(nmp):
        near = step(dq, "mp", by) if by else dq
        part += lax.dot_general(near, fans[by], BOTH_LAST, preferred_element_type=F32).astype(BF16).astype(F32)
    part = part.astype(BF16)
    attended = jnp.concatenate([jnp.zeros((LEAD, width), BF16), out[:real]], 0)
    input_grad = jnp.concatenate([jnp.zeros((SKIP, d // nmp), BF16), part], 0)
    return attended[None], input_grad[None], query_grad


def solution(mesh):
    fine = Mesh(mesh.devices.reshape(4, 8, 2, 4), ("x", "z", "core", "mp"))
    return jax.shard_map(
        local,
        mesh=fine,
        in_specs=(
            P(DP, None, None),
            P(None, "mp"),
            P(DP, None, None, "mp"),
            P(DP, None, None),
            P(DP, None, None),
            P(DP, None, "mp"),
        ),
        out_specs=(P(DP, None, "mp"), P(DP, None, "mp"), P(DP, "mp")),
        check_vma=False,
    )
```

```python
import functools

import jax
import jax.numpy as jnp
from jax import lax
from jax.experimental import pallas as pl
from jax.experimental.pallas import tpu as pltpu
from jax.sharding import Mesh
from jax.sharding import PartitionSpec as P

HEAD_DIM = 128
STRETCH = 64
LEAD = STRETCH - 1
TILE = 16
SKIP = LEAD // TILE * TILE
DP = ("x", "z", "core")
VMEM = 32 << 20
BF16, F32 = jnp.bfloat16, jnp.float32
BOTH_LAST = (((1,), (1,)), ((), ()))
BOTH_FIRST = (((0,), (0,)), ((), ()))


def cut_kernel(owner_ref, row_ref, cache_ref, out_ref, named_ref):
    rows = cache_ref.shape[0]
    stretches, neigh = owner_ref.shape
    named_ref[...] = jnp.zeros_like(named_ref)
    named_ref[:stretches, :neigh] = owner_ref[...].astype(F32)
    named_ref[stretches : 2 * stretches, :neigh] = row_ref[...].astype(F32)
    _, heads, tiles, _, _, _ = out_ref.shape
    for head in range(heads):
        cols = slice(head * HEAD_DIM, (head + 1) * HEAD_DIM)
        for tile in range(tiles):
            out_ref[0, head, tile, :rows] = cache_ref[:, 0, tile * TILE : (tile + 1) * TILE, cols]
            out_ref[0, head, tile, rows] = named_ref[...].astype(BF16)


def cut(nb_owner, nb_row, cache):
    rows, _, nb_len, width = cache.shape
    tiles, heads, parts = nb_len // TILE, width // HEAD_DIM, 2
    named = pl.BlockSpec(nb_owner.shape, lambda a, t: (0, 0))
    return pl.pallas_call(
        cut_kernel,
        grid=(2, parts),
        in_specs=[
            named,
            named,
            pl.BlockSpec((rows, 1, nb_len // parts, width), lambda a, t: (0, a, t, 0)),
        ],
        out_specs=pl.BlockSpec(
            (1, heads, tiles // parts, rows + 1, TILE, HEAD_DIM), lambda a, t: (a, 0, t, 0, 0, 0)
        ),
        out_shape=jax.ShapeDtypeStruct((2, heads, tiles, rows + 1, TILE, HEAD_DIM), BF16),
        scratch_shapes=[pltpu.VMEM((TILE, HEAD_DIM), F32)],
        compiler_params=pltpu.CompilerParams(vmem_limit_bytes=VMEM),
        cost_estimate=pl.CostEstimate(flops=0, bytes_accessed=4 << 20, transcendentals=0),
        name="cut",
    )(nb_owner, nb_row, cache).reshape(-1, rows + 1, TILE, HEAD_DIM)


def pick_kernel(ids_ref, tiles_ref, out_ref, *, slots):
    base = pl.program_id(0) * slots
    for slot in range(slots):
        out_ref[slot] = tiles_ref[ids_ref[base + slot]]


def pick(ids, tiles):
    count, slots = ids.shape[0], 64
    return pl.pallas_call(
        functools.partial(pick_kernel, slots=slots),
        grid_spec=pltpu.PrefetchScalarGridSpec(
            num_scalar_prefetch=1,
            grid=(count // slots,),
            in_specs=[pl.BlockSpec(tiles.shape, lambda s, ids: (0, 0, 0))],
            out_specs=pl.BlockSpec((slots,) + tiles.shape[1:], lambda s, ids: (s, 0, 0)),
        ),
        out_shape=jax.ShapeDtypeStruct((count,) + tiles.shape[1:], tiles.dtype),
        compiler_params=pltpu.CompilerParams(vmem_limit_bytes=VMEM),
        cost_estimate=pl.CostEstimate(flops=0, bytes_accessed=6 << 20, transcendentals=0),
        name="pick",
    )(ids, tiles)


def attend_kernel(q_ref, g_ref, kv_ref, out_ref, dq_ref, *, heads):
    scale = HEAD_DIM ** (-0.5)
    cols = [slice(h * HEAD_DIM, (h + 1) * HEAD_DIM) for h in range(heads)]
    keys = [kv_ref[0, h].reshape(-1, HEAD_DIM) for h in range(heads)]
    values = [kv_ref[1, h].reshape(-1, HEAD_DIM) for h in range(heads)]
    scores = [
        lax.dot_general(q_ref[:, c], k, BOTH_LAST, preferred_element_type=F32)
        for c, k in zip(cols, keys)
    ]
    dprobs = [
        lax.dot_general(g_ref[:, c], v, BOTH_LAST, preferred_element_type=F32)
        for c, v in zip(cols, values)
    ]
    probs, dscores = [], []
    for score, dprob in zip(scores, dprobs):
        score = score * scale
        exps = jnp.exp(score - jnp.max(score, axis=-1, keepdims=True))
        prob = exps * (1.0 / jnp.sum(exps, axis=-1, keepdims=True))
        delta = jnp.sum(dprob * prob, axis=-1, keepdims=True)
        probs.append(prob.astype(BF16))
        dscores.append((prob * (dprob - delta) * scale).astype(BF16))
    for c, k, v, prob, dscore in zip(cols, keys, values, probs, dscores):
        out_ref[:, c] = jnp.dot(prob, v, preferred_element_type=F32).astype(BF16)
        dq_ref[:, c] = jnp.dot(dscore, k, preferred_element_type=F32).astype(BF16)


def attend(q, g, kv, neigh):
    rows, width = q.shape
    count = rows // STRETCH
    _, heads, tiles, slots, _, _ = kv.shape
    block = pl.BlockSpec((STRETCH, width), lambda c: (c, 0))
    return pl.pallas_call(
        functools.partial(attend_kernel, heads=heads),
        grid=(count,),
        in_specs=[
            block,
            block,
            pl.BlockSpec((2, heads, tiles, neigh, TILE, HEAD_DIM), lambda c: (0, 0, 0, c, 0, 0)),
        ],
        out_specs=[block, block],
        out_shape=[jax.ShapeDtypeStruct(q.shape, BF16)] * 2,
        compiler_params=pltpu.CompilerParams(vmem_limit_bytes=VMEM),
        cost_estimate=pl.CostEstimate(
            flops=10 * rows * width * neigh * tiles * TILE, bytes_accessed=kv.size * 2, transcendentals=0
        ),
        name="attend",
    )(q, g, kv)


def step(array, axis, by):
    size = lax.axis_size(axis)
    return lax.ppermute(array, axis, [(i, (i + by) % size) for i in range(size)])


def local(inputs, w_query, cache_kv, nb_owner, nb_row, out_grad):
    nx, nz, nc = (lax.axis_size(a) for a in DP)
    ndp, nmp = nx * nz * nc, lax.axis_size("mp")
    mx, mz, mc = (lax.axis_index(a) for a in DP)
    my = lax.axis_index("mp")
    tokens, grad_rows = inputs[0], out_grad[0]
    length, d = tokens.shape
    width = w_query.shape[1]
    heads = width // HEAD_DIM
    db_rows, _, nb_len, _ = cache_kv.shape
    _, stretches, neigh = nb_owner.shape
    requests = stretches * neigh
    tiles = nb_len // TILE
    real = length - LEAD

    message = cut(nb_owner[0], nb_row[0], cache_kv)
    held = lax.all_to_all(message, DP, split_axis=0, concat_axis=0, tiled=True)

    block = d // nmp
    fans = [lax.dynamic_slice(w_query, ((my + by) % nmp * block, 0), (block, width)) for by in range(nmp)]
    fans = [step(a, "mp", by) if by else a for by, a in enumerate(fans)]
    held, fans = lax.optimization_barrier((held, fans))

    named = held[:, db_rows, : 2 * stretches, :neigh].astype(jnp.int32)
    ids = named[:, :stretches] * (db_rows + 1) + named[:, stretches:]
    send = pick(ids.reshape(-1), held.reshape(-1, TILE, HEAD_DIM))
    got = lax.all_to_all(
        send.reshape(ndp, requests, TILE, HEAD_DIM), DP, split_axis=0, concat_axis=0, tiled=True
    )

    late, weights, grad_rows, _ = lax.optimization_barrier((tokens, w_query, grad_rows, held))
    block = d // nx
    share = [lax.dynamic_slice(late, (SKIP, (mx + by) % nx * block), (length - SKIP, block)) for by in range(nx)]
    share = [step(a, "x", by) if by else a for by, a in enumerate(share)]

    def shifted(array):
        return jnp.concatenate([array[LEAD:], jnp.zeros((LEAD, array.shape[1]), array.dtype)], 0)

    q = shifted(jnp.dot(late, weights, preferred_element_type=F32).astype(BF16))
    g = shifted(grad_rows)
    got, share, q, g = lax.optimization_barrier((got, share, q, g))

    out, dq = attend(q, g, got.reshape(2, heads, tiles, requests, TILE, HEAD_DIM), neigh)
    dq = jnp.concatenate([jnp.zeros((LEAD - SKIP, width), BF16), dq[:real]], 0)

    total = 0.0
    for by in range(nx):
        near = step(dq, "x", by) if by else dq
        total += lax.dot_general(share[by], near, BOTH_FIRST, preferred_element_type=F32)
    total = total.reshape(nz, nc, -1, width)
    mine = lax.dynamic_index_in_dim(total, mc, 1, keepdims=False)
    mine += step(lax.dynamic_index_in_dim(total, 1 - mc, 1, keepdims=False), "core", 1)
    query_grad = lax.dynamic_index_in_dim(mine, mz, 0, keepdims=False)
    for by in range(1, nz):
        query_grad += step(lax.dynamic_index_in_dim(mine, (mz + by) % nz, 0, keepdims=False), "z", by)

    part = 0.0
    for by in range(nmp):
        near = step(dq, "mp", by) if by else dq
        part += lax.dot_general(near, fans[by], BOTH_LAST, preferred_element_type=F32).astype(BF16).astype(F32)
    part = part.astype(BF16)
    attended = jnp.concatenate([jnp.zeros((LEAD, width), BF16), out[:real]], 0)
    input_grad = jnp.concatenate([jnp.zeros((SKIP, d // nmp), BF16), part], 0)
    return attended[None], input_grad[None], query_grad


def solution(mesh):
    fine = Mesh(mesh.devices.reshape(4, 8, 2, 4), ("x", "z", "core", "mp"))
    return jax.shard_map(
        local,
        mesh=fine,
        in_specs=(
            P(DP, None, None),
            P(None, "mp"),
            P(DP, None, None, "mp"),
            P(DP, None, None),
            P(DP, None, None),
            P(DP, None, "mp"),
        ),
        out_specs=(P(DP, None, "mp"), P(DP, None, "mp"), P(DP, "mp")),
        check_vma=False,
    )
```

```python
import functools

import jax
import jax.numpy as jnp
from jax import lax
from jax.experimental import pallas as pl
from jax.experimental.pallas import tpu as pltpu
from jax.sharding import Mesh
from jax.sharding import PartitionSpec as P

HEAD_DIM = 128
STRETCH = 64
LEAD = STRETCH - 1
TILE = 16
SKIP = LEAD // TILE * TILE
DP = ("x", "z", "core")
VMEM = 32 << 20
BF16, F32 = jnp.bfloat16, jnp.float32
BOTH_LAST = (((1,), (1,)), ((), ()))
BOTH_FIRST = (((0,), (0,)), ((), ()))


def cut_kernel(owner_ref, row_ref, cache_ref, out_ref, named_ref):
    rows = cache_ref.shape[0]
    _, stretches, neigh = owner_ref.shape
    named_ref[...] = jnp.zeros_like(named_ref)
    named_ref[:stretches, :neigh] = owner_ref[0].astype(F32)
    named_ref[stretches : 2 * stretches, :neigh] = row_ref[0].astype(F32)
    _, heads, tiles, _, _, _ = out_ref.shape
    for head in range(heads):
        cols = slice(head * HEAD_DIM, (head + 1) * HEAD_DIM)
        for tile in range(tiles):
            out_ref[0, head, tile, :rows] = cache_ref[:, 0, tile * TILE : (tile + 1) * TILE, cols]
            out_ref[0, head, tile, rows] = named_ref[...].astype(BF16)


def cut(nb_owner, nb_row, cache):
    rows, _, nb_len, width = cache.shape
    tiles, heads, parts = nb_len // TILE, width // HEAD_DIM, 2
    named = pl.BlockSpec(nb_owner.shape, lambda a, t: (0, 0, 0))
    return pl.pallas_call(
        cut_kernel,
        grid=(2, parts),
        in_specs=[
            named,
            named,
            pl.BlockSpec((rows, 1, nb_len // parts, width), lambda a, t: (0, a, t, 0)),
        ],
        out_specs=pl.BlockSpec(
            (1, heads, tiles // parts, rows + 1, TILE, HEAD_DIM), lambda a, t: (a, 0, t, 0, 0, 0)
        ),
        out_shape=jax.ShapeDtypeStruct((2, heads, tiles, rows + 1, TILE, HEAD_DIM), BF16),
        scratch_shapes=[pltpu.VMEM((TILE, HEAD_DIM), F32)],
        compiler_params=pltpu.CompilerParams(vmem_limit_bytes=VMEM),
        cost_estimate=pl.CostEstimate(flops=0, bytes_accessed=4 << 20, transcendentals=0),
        name="cut",
    )(nb_owner, nb_row, cache).reshape(-1, rows + 1, TILE, HEAD_DIM)


def pick_kernel(ids_ref, tiles_ref, out_ref, *, slots):
    base = pl.program_id(0) * slots
    for slot in range(slots):
        out_ref[slot] = tiles_ref[ids_ref[base + slot]]


def pick(ids, tiles):
    count, slots = ids.shape[0], 64
    return pl.pallas_call(
        functools.partial(pick_kernel, slots=slots),
        grid_spec=pltpu.PrefetchScalarGridSpec(
            num_scalar_prefetch=1,
            grid=(count // slots,),
            in_specs=[pl.BlockSpec(tiles.shape, lambda s, ids: (0, 0, 0))],
            out_specs=pl.BlockSpec((slots,) + tiles.shape[1:], lambda s, ids: (s, 0, 0)),
        ),
        out_shape=jax.ShapeDtypeStruct((count,) + tiles.shape[1:], tiles.dtype),
        compiler_params=pltpu.CompilerParams(vmem_limit_bytes=VMEM),
        cost_estimate=pl.CostEstimate(flops=0, bytes_accessed=6 << 20, transcendentals=0),
        name="pick",
    )(ids, tiles)


def attend_kernel(q_ref, g_ref, kv_ref, out_ref, dq_ref, *, heads):
    scale = HEAD_DIM ** (-0.5)
    cols = [slice(h * HEAD_DIM, (h + 1) * HEAD_DIM) for h in range(heads)]
    keys = [kv_ref[0, h].reshape(-1, HEAD_DIM) for h in range(heads)]
    values = [kv_ref[1, h].reshape(-1, HEAD_DIM) for h in range(heads)]
    scores = [
        lax.dot_general(q_ref[:, c], k, BOTH_LAST, preferred_element_type=F32)
        for c, k in zip(cols, keys)
    ]
    dprobs = [
        lax.dot_general(g_ref[:, c], v, BOTH_LAST, preferred_element_type=F32)
        for c, v in zip(cols, values)
    ]
    probs, dscores = [], []
    for score, dprob in zip(scores, dprobs):
        score = score * scale
        exps = jnp.exp(score - jnp.max(score, axis=-1, keepdims=True))
        prob = exps * (1.0 / jnp.sum(exps, axis=-1, keepdims=True))
        delta = jnp.sum(dprob * prob, axis=-1, keepdims=True)
        probs.append(prob.astype(BF16))
        dscores.append((prob * (dprob - delta) * scale).astype(BF16))
    for c, k, v, prob, dscore in zip(cols, keys, values, probs, dscores):
        out_ref[:, c] = jnp.dot(prob, v, preferred_element_type=F32).astype(BF16)
        dq_ref[:, c] = jnp.dot(dscore, k, preferred_element_type=F32).astype(BF16)


def attend(q, g, kv, neigh):
    rows, width = q.shape
    count = rows // STRETCH
    _, heads, tiles, slots, _, _ = kv.shape
    block = pl.BlockSpec((STRETCH, width), lambda c: (c, 0))
    return pl.pallas_call(
        functools.partial(attend_kernel, heads=heads),
        grid=(count,),
        in_specs=[
            block,
            block,
            pl.BlockSpec((2, heads, tiles, neigh, TILE, HEAD_DIM), lambda c: (0, 0, 0, c, 0, 0)),
        ],
        out_specs=[block, block],
        out_shape=[jax.ShapeDtypeStruct(q.shape, BF16)] * 2,
        compiler_params=pltpu.CompilerParams(vmem_limit_bytes=VMEM),
        cost_estimate=pl.CostEstimate(
            flops=10 * rows * width * neigh * tiles * TILE, bytes_accessed=kv.size * 2, transcendentals=0
        ),
        name="attend",
    )(q, g, kv)


def step(array, axis, by):
    size = lax.axis_size(axis)
    return lax.ppermute(array, axis, [(i, (i + by) % size) for i in range(size)])


def local(inputs, w_query, cache_kv, nb_owner, nb_row, out_grad):
    nx, nz, nc = (lax.axis_size(a) for a in DP)
    ndp, nmp = nx * nz * nc, lax.axis_size("mp")
    mx, mz, mc = (lax.axis_index(a) for a in DP)
    my = lax.axis_index("mp")
    tokens, grad_rows = inputs[0], out_grad[0]
    length, d = tokens.shape
    width = w_query.shape[1]
    heads = width // HEAD_DIM
    db_rows, _, nb_len, _ = cache_kv.shape
    _, stretches, neigh = nb_owner.shape
    requests = stretches * neigh
    tiles = nb_len // TILE
    real = length - LEAD

    message = cut(nb_owner, nb_row, cache_kv)
    held = lax.all_to_all(message, DP, split_axis=0, concat_axis=0, tiled=True)

    block = d // nmp
    fans = [lax.dynamic_slice(w_query, ((my + by) % nmp * block, 0), (block, width)) for by in range(nmp)]
    fans = [step(a, "mp", by) if by else a for by, a in enumerate(fans)]
    held, fans = lax.optimization_barrier((held, fans))

    named = held[:, db_rows, : 2 * stretches, :neigh].astype(jnp.int32)
    ids = named[:, :stretches] * (db_rows + 1) + named[:, stretches:]
    send = pick(ids.reshape(-1), held.reshape(-1, TILE, HEAD_DIM))
    got = lax.all_to_all(
        send.reshape(ndp, requests, TILE, HEAD_DIM), DP, split_axis=0, concat_axis=0, tiled=True
    )

    late, weights, grad_rows, _ = lax.optimization_barrier((tokens, w_query, grad_rows, held))
    block = d // nx
    share = [lax.dynamic_slice(late, (SKIP, (mx + by) % nx * block), (length - SKIP, block)) for by in range(nx)]
    share = [step(a, "x", by) if by else a for by, a in enumerate(share)]

    def shifted(array):
        return jnp.concatenate([array[LEAD:], jnp.zeros((LEAD, array.shape[1]), array.dtype)], 0)

    q = shifted(jnp.dot(late, weights, preferred_element_type=F32).astype(BF16))
    g = shifted(grad_rows)
    got, share, q, g = lax.optimization_barrier((got, share, q, g))

    out, dq = attend(q, g, got.reshape(2, heads, tiles, requests, TILE, HEAD_DIM), neigh)
    dq = jnp.concatenate([jnp.zeros((LEAD - SKIP, width), BF16), dq[:real]], 0)

    total = 0.0
    for by in range(nx):
        near = step(dq, "x", by) if by else dq
        total += lax.dot_general(share[by], near, BOTH_FIRST, preferred_element_type=F32)
    total = total.reshape(nz, nc, -1, width)
    mine = lax.dynamic_index_in_dim(total, mc, 1, keepdims=False)
    mine += step(lax.dynamic_index_in_dim(total, 1 - mc, 1, keepdims=False), "core", 1)
    groups = jnp.broadcast_to(dq[None], (nmp,) + dq.shape)
    groups = lax.all_to_all(groups, "mp", split_axis=0, concat_axis=0, tiled=True)
    groups, mine = lax.optimization_barrier((groups, mine))
    terms = [lax.dynamic_index_in_dim(mine, (mz + by) % nz, 0, keepdims=False) for by in range(nz)]
    terms = [step(a, "z", by) if by else a for by, a in enumerate(terms)]

    groups, terms[1] = lax.optimization_barrier((groups, terms[1]))
    query_grad = sum(terms)
    part = 0.0
    for by in range(nmp):
        near = lax.dynamic_index_in_dim(groups, (my - by) % nmp, 0, keepdims=False)
        part += lax.dot_general(near, fans[by], BOTH_LAST, preferred_element_type=F32).astype(BF16).astype(F32)
    part = part.astype(BF16)
    attended = jnp.concatenate([jnp.zeros((LEAD, width), BF16), out[:real]], 0)
    input_grad = jnp.concatenate([jnp.zeros((SKIP, d // nmp), BF16), part], 0)
    return attended[None], input_grad[None], query_grad


def solution(mesh):
    fine = Mesh(mesh.devices.reshape(4, 8, 2, 4), ("x", "z", "core", "mp"))
    return jax.shard_map(
        local,
        mesh=fine,
        in_specs=(
            P(DP, None, None),
            P(None, "mp"),
            P(DP, None, None, "mp"),
            P(DP, None, None),
            P(DP, None, None),
            P(DP, None, "mp"),
        ),
        out_specs=(P(DP, None, "mp"), P(DP, None, "mp"), P(DP, "mp")),
        check_vma=False,
    )
```

```python
import functools

import jax
import jax.numpy as jnp
from jax import lax
from jax.experimental import pallas as pl
from jax.experimental.pallas import tpu as pltpu
from jax.sharding import Mesh
from jax.sharding import PartitionSpec as P

HEAD_DIM = 128
STRETCH = 64
LEAD = STRETCH - 1
TILE = 16
SKIP = LEAD // TILE * TILE
DP = ("x", "z", "core")
VMEM = 32 << 20
BF16, F32 = jnp.bfloat16, jnp.float32
BOTH_LAST = (((1,), (1,)), ((), ()))
BOTH_FIRST = (((0,), (0,)), ((), ()))


def cut_kernel(owner_ref, row_ref, cache_ref, out_ref, owners_ref, rows_ref):
    rows = cache_ref.shape[0]
    _, stretches, neigh = owner_ref.shape
    owners_ref[...] = jnp.zeros_like(owners_ref)
    rows_ref[...] = jnp.zeros_like(rows_ref)
    owners_ref[:, :neigh] = owner_ref[0].astype(F32)
    rows_ref[:, :neigh] = row_ref[0].astype(F32)
    named = (owners_ref[...] + pltpu.roll(rows_ref[...], neigh, 1)).astype(BF16)
    _, heads, tiles, _, _ = out_ref.shape
    for head in range(heads):
        cols = slice(head * HEAD_DIM, (head + 1) * HEAD_DIM)
        for tile in range(tiles):
            for row in range(rows):
                out_ref[0, head, tile, row * TILE : (row + 1) * TILE] = cache_ref[
                    row, 0, tile * TILE : (tile + 1) * TILE, cols
                ]
            out_ref[0, head, tile, rows * TILE :] = named


def cut(nb_owner, nb_row, cache):
    rows, _, nb_len, width = cache.shape
    tiles, heads, parts = nb_len // TILE, width // HEAD_DIM, 2
    stretches = nb_owner.shape[1]
    high = rows * TILE + stretches
    named = pl.BlockSpec(nb_owner.shape, lambda a, t: (0, 0, 0))
    return pl.pallas_call(
        cut_kernel,
        grid=(2, parts),
        in_specs=[
            named,
            named,
            pl.BlockSpec((rows, 1, nb_len // parts, width), lambda a, t: (0, a, t, 0)),
        ],
        out_specs=pl.BlockSpec(
            (1, heads, tiles // parts, high, HEAD_DIM), lambda a, t: (a, 0, t, 0, 0)
        ),
        out_shape=jax.ShapeDtypeStruct((2, heads, tiles, high, HEAD_DIM), BF16),
        scratch_shapes=[pltpu.VMEM((stretches, HEAD_DIM), F32)] * 2,
        compiler_params=pltpu.CompilerParams(vmem_limit_bytes=VMEM),
        cost_estimate=pl.CostEstimate(flops=0, bytes_accessed=4 << 20, transcendentals=0),
        name="cut",
    )(nb_owner, nb_row, cache).reshape(-1, high, HEAD_DIM)


def pick_kernel(ids_ref, held_ref, out_ref, *, slots, rows):
    base = pl.program_id(0) * slots
    for slot in range(slots):
        named = ids_ref[base + slot]
        at = pl.multiple_of(named % rows * TILE, TILE)
        out_ref[slot] = held_ref[named // rows, pl.ds(at, TILE)]


def pick(ids, held, rows):
    count, slots = ids.shape[0], 64
    return pl.pallas_call(
        functools.partial(pick_kernel, slots=slots, rows=rows),
        grid_spec=pltpu.PrefetchScalarGridSpec(
            num_scalar_prefetch=1,
            grid=(count // slots,),
            in_specs=[pl.BlockSpec(held.shape, lambda s, ids: (0, 0, 0))],
            out_specs=pl.BlockSpec((slots, TILE, HEAD_DIM), lambda s, ids: (s, 0, 0)),
        ),
        out_shape=jax.ShapeDtypeStruct((count, TILE, HEAD_DIM), BF16),
        compiler_params=pltpu.CompilerParams(vmem_limit_bytes=VMEM),
        cost_estimate=pl.CostEstimate(flops=0, bytes_accessed=6 << 20, transcendentals=0),
        name="pick",
    )(ids, held)


def attend_kernel(q_ref, g_ref, kv_ref, out_ref, dq_ref, *, heads):
    scale = HEAD_DIM ** (-0.5)
    cols = [slice(h * HEAD_DIM, (h + 1) * HEAD_DIM) for h in range(heads)]
    keys = [kv_ref[0, h].reshape(-1, HEAD_DIM) for h in range(heads)]
    values = [kv_ref[1, h].reshape(-1, HEAD_DIM) for h in range(heads)]
    scores = [
        lax.dot_general(q_ref[:, c], k, BOTH_LAST, preferred_element_type=F32)
        for c, k in zip(cols, keys)
    ]
    dprobs = [
        lax.dot_general(g_ref[:, c], v, BOTH_LAST, preferred_element_type=F32)
        for c, v in zip(cols, values)
    ]
    probs, dscores = [], []
    for score, dprob in zip(scores, dprobs):
        score = score * scale
        exps = jnp.exp(score - jnp.max(score, axis=-1, keepdims=True))
        prob = exps * (1.0 / jnp.sum(exps, axis=-1, keepdims=True))
        delta = jnp.sum(dprob * prob, axis=-1, keepdims=True)
        probs.append(prob.astype(BF16))
        dscores.append((prob * (dprob - delta) * scale).astype(BF16))
    for c, k, v, prob, dscore in zip(cols, keys, values, probs, dscores):
        out_ref[:, c] = jnp.dot(prob, v, preferred_element_type=F32).astype(BF16)
        dq_ref[:, c] = jnp.dot(dscore, k, preferred_element_type=F32).astype(BF16)


def attend(q, g, kv, neigh):
    rows, width = q.shape
    count = rows // STRETCH
    _, heads, tiles, slots, _, _ = kv.shape
    block = pl.BlockSpec((STRETCH, width), lambda c: (c, 0))
    return pl.pallas_call(
        functools.partial(attend_kernel, heads=heads),
        grid=(count,),
        in_specs=[
            block,
            block,
            pl.BlockSpec((2, heads, tiles, neigh, TILE, HEAD_DIM), lambda c: (0, 0, 0, c, 0, 0)),
        ],
        out_specs=[block, block],
        out_shape=[jax.ShapeDtypeStruct(q.shape, BF16)] * 2,
        compiler_params=pltpu.CompilerParams(vmem_limit_bytes=VMEM),
        cost_estimate=pl.CostEstimate(
            flops=10 * rows * width * neigh * tiles * TILE, bytes_accessed=kv.size * 2, transcendentals=0
        ),
        name="attend",
    )(q, g, kv)


def step(array, axis, by):
    size = lax.axis_size(axis)
    return lax.ppermute(array, axis, [(i, (i + by) % size) for i in range(size)])


def local(inputs, w_query, cache_kv, nb_owner, nb_row, out_grad):
    nx, nz, nc = (lax.axis_size(a) for a in DP)
    ndp, nmp = nx * nz * nc, lax.axis_size("mp")
    mx, mz, mc = (lax.axis_index(a) for a in DP)
    my = lax.axis_index("mp")
    tokens, grad_rows = inputs[0], out_grad[0]
    length, d = tokens.shape
    width = w_query.shape[1]
    heads = width // HEAD_DIM
    db_rows, _, nb_len, _ = cache_kv.shape
    _, stretches, neigh = nb_owner.shape
    requests = stretches * neigh
    tiles = nb_len // TILE
    real = length - LEAD

    message = cut(nb_owner, nb_row, cache_kv)
    held = lax.all_to_all(message, DP, split_axis=0, concat_axis=0, tiled=True)

    block = d // nmp
    fans = [lax.dynamic_slice(w_query, ((my + by) % nmp * block, 0), (block, width)) for by in range(nmp)]
    fans = [step(a, "mp", by) if by else a for by, a in enumerate(fans)]
    held, fans = lax.optimization_barrier((held, fans))

    named = held[:, db_rows * TILE :, : 2 * neigh].astype(jnp.int32)
    ids = named[..., :neigh] * db_rows + named[..., neigh:]
    send = pick(ids.reshape(-1), held, db_rows)
    got = lax.all_to_all(
        send.reshape(ndp, requests, TILE, HEAD_DIM), DP, split_axis=0, concat_axis=0, tiled=True
    )

    late, weights, grad_rows, _ = lax.optimization_barrier((tokens, w_query, grad_rows, held))
    block = d // nx
    share = [lax.dynamic_slice(late, (SKIP, (mx + by) % nx * block), (length - SKIP, block)) for by in range(nx)]
    share = [step(a, "x", by) if by else a for by, a in enumerate(share)]

    def ordered(array):
        array = array.T.reshape(nz, nc, -1, array.shape[0])
        array = jnp.concatenate([array, array], 0)
        array = lax.dynamic_slice_in_dim(array, mz, nz, 0)
        own = lax.dynamic_index_in_dim(array, mc, 1, keepdims=False)
        other = lax.dynamic_index_in_dim(array, 1 - mc, 1, keepdims=False)
        return [a.reshape(-1, a.shape[-1]) for a in (own, other)]

    share = [ordered(a) for a in share]

    def shifted(array):
        return jnp.concatenate([array[LEAD:], jnp.zeros((LEAD, array.shape[1]), array.dtype)], 0)

    q = shifted(jnp.dot(late, weights, preferred_element_type=F32).astype(BF16))
    g = shifted(grad_rows)
    got, share, q, g = lax.optimization_barrier((got, share, q, g))

    out, dq = attend(q, g, got.reshape(2, heads, tiles, requests, TILE, HEAD_DIM), neigh)
    dq = jnp.concatenate([jnp.zeros((LEAD - SKIP, width), BF16), dq[:real]], 0)

    mine = other = 0.0
    for by in range(nx):
        near = step(dq, "x", by) if by else dq
        other += jnp.dot(share[by][1], near, preferred_element_type=F32)
        mine += jnp.dot(share[by][0], near, preferred_element_type=F32)
    mine += step(other, "core", 1)
    groups = jnp.broadcast_to(dq[None], (nmp,) + dq.shape)
    groups = lax.all_to_all(groups, "mp", split_axis=0, concat_axis=0, tiled=True)
    groups, mine = lax.optimization_barrier((groups, mine))
    terms = jnp.split(mine, nz)
    terms = [step(a, "z", by) if by else a for by, a in enumerate(terms)]

    groups, terms[1] = lax.optimization_barrier((groups, terms[1]))
    query_grad = sum(terms)
    part = 0.0
    for by in range(nmp):
        near = lax.dynamic_index_in_dim(groups, (my - by) % nmp, 0, keepdims=False)
        part += lax.dot_general(near, fans[by], BOTH_LAST, preferred_element_type=F32).astype(BF16).astype(F32)
    part = part.astype(BF16)
    attended = jnp.concatenate([jnp.zeros((LEAD, width), BF16), out[:real]], 0)
    input_grad = jnp.concatenate([jnp.zeros((SKIP, d // nmp), BF16), part], 0)
    return attended[None], input_grad[None], query_grad


def solution(mesh):
    fine = Mesh(mesh.devices.reshape(4, 8, 2, 4), ("x", "z", "core", "mp"))
    return jax.shard_map(
        local,
        mesh=fine,
        in_specs=(
            P(DP, None, None),
            P(None, "mp"),
            P(DP, None, None, "mp"),
            P(DP, None, None),
            P(DP, None, None),
            P(DP, None, "mp"),
        ),
        out_specs=(P(DP, None, "mp"), P(DP, None, "mp"), P(DP, "mp")),
        check_vma=False,
    )
```

```python
import functools

import jax
import jax.numpy as jnp
from jax import lax
from jax.experimental import pallas as pl
from jax.experimental.pallas import tpu as pltpu
from jax.sharding import Mesh
from jax.sharding import PartitionSpec as P

HEAD_DIM = 128
STRETCH = 64
LEAD = STRETCH - 1
TILE = 16
SKIP = LEAD // TILE * TILE
DP = ("x", "z", "core")
VMEM = 32 << 20
BF16, F32 = jnp.bfloat16, jnp.float32
BOTH_LAST = (((1,), (1,)), ((), ()))
BOTH_FIRST = (((0,), (0,)), ((), ()))


def cut_kernel(owner_ref, row_ref, cache_ref, out_ref, named_ref):
    rows = cache_ref.shape[0]
    _, stretches, neigh = owner_ref.shape
    named_ref[...] = jnp.zeros_like(named_ref)
    named_ref[:stretches, :neigh] = owner_ref[0].astype(F32)
    named_ref[stretches : 2 * stretches, :neigh] = row_ref[0].astype(F32)
    _, heads, tiles, _, _, _ = out_ref.shape
    for head in range(heads):
        cols = slice(head * HEAD_DIM, (head + 1) * HEAD_DIM)
        for tile in range(tiles):
            out_ref[0, head, tile, :rows] = cache_ref[:, 0, tile * TILE : (tile + 1) * TILE, cols]
            out_ref[0, head, tile, rows] = named_ref[...].astype(BF16)


def cut(nb_owner, nb_row, cache):
    rows, _, nb_len, width = cache.shape
    tiles, heads, parts = nb_len // TILE, width // HEAD_DIM, 2
    named = pl.BlockSpec(nb_owner.shape, lambda a, t: (0, 0, 0))
    return pl.pallas_call(
        cut_kernel,
        grid=(2, parts),
        in_specs=[
            named,
            named,
            pl.BlockSpec((rows, 1, nb_len // parts, width), lambda a, t: (0, a, t, 0)),
        ],
        out_specs=pl.BlockSpec(
            (1, heads, tiles // parts, rows + 1, TILE, HEAD_DIM), lambda a, t: (a, 0, t, 0, 0, 0)
        ),
        out_shape=jax.ShapeDtypeStruct((2, heads, tiles, rows + 1, TILE, HEAD_DIM), BF16),
        scratch_shapes=[pltpu.VMEM((TILE, HEAD_DIM), F32)],
        compiler_params=pltpu.CompilerParams(vmem_limit_bytes=VMEM),
        cost_estimate=pl.CostEstimate(flops=0, bytes_accessed=4 << 20, transcendentals=0),
        name="cut",
    )(nb_owner, nb_row, cache).reshape(-1, rows + 1, TILE, HEAD_DIM)


def pick_kernel(ids_ref, tiles_ref, out_ref, *, slots):
    base = pl.program_id(0) * slots
    for slot in range(slots):
        out_ref[slot] = tiles_ref[ids_ref[base + slot]]


def pick(ids, tiles):
    count, slots = ids.shape[0], 64
    return pl.pallas_call(
        functools.partial(pick_kernel, slots=slots),
        grid_spec=pltpu.PrefetchScalarGridSpec(
            num_scalar_prefetch=1,
            grid=(count // slots,),
            in_specs=[pl.BlockSpec(tiles.shape, lambda s, ids: (0, 0, 0))],
            out_specs=pl.BlockSpec((slots,) + tiles.shape[1:], lambda s, ids: (s, 0, 0)),
        ),
        out_shape=jax.ShapeDtypeStruct((count,) + tiles.shape[1:], tiles.dtype),
        compiler_params=pltpu.CompilerParams(vmem_limit_bytes=VMEM),
        cost_estimate=pl.CostEstimate(flops=0, bytes_accessed=6 << 20, transcendentals=0),
        name="pick",
    )(ids, tiles)


def attend_kernel(q_ref, g_ref, kv_ref, out_ref, dq_ref, *, heads):
    scale = HEAD_DIM ** (-0.5)
    cols = [slice(h * HEAD_DIM, (h + 1) * HEAD_DIM) for h in range(heads)]
    keys = [kv_ref[0, h].reshape(-1, HEAD_DIM) for h in range(heads)]
    values = [kv_ref[1, h].reshape(-1, HEAD_DIM) for h in range(heads)]
    scores = [
        lax.dot_general(q_ref[:, c], k, BOTH_LAST, preferred_element_type=F32)
        for c, k in zip(cols, keys)
    ]
    dprobs = [
        lax.dot_general(g_ref[:, c], v, BOTH_LAST, preferred_element_type=F32)
        for c, v in zip(cols, values)
    ]
    probs, dscores = [], []
    for score, dprob in zip(scores, dprobs):
        score = score * scale
        exps = jnp.exp(score - jnp.max(score, axis=-1, keepdims=True))
        prob = exps * (1.0 / jnp.sum(exps, axis=-1, keepdims=True))
        delta = jnp.sum(dprob * prob, axis=-1, keepdims=True)
        probs.append(prob.astype(BF16))
        dscores.append((prob * (dprob - delta) * scale).astype(BF16))
    for c, k, v, prob, dscore in zip(cols, keys, values, probs, dscores):
        out_ref[:, c] = jnp.dot(prob, v, preferred_element_type=F32).astype(BF16)
        dq_ref[:, c] = jnp.dot(dscore, k, preferred_element_type=F32).astype(BF16)


def attend(q, g, kv, neigh, first):
    rows, width = q.shape
    count = rows // STRETCH
    _, heads, tiles, slots, _, _ = kv.shape
    block = pl.BlockSpec((STRETCH, width), lambda c: (c, 0))
    return pl.pallas_call(
        functools.partial(attend_kernel, heads=heads),
        grid=(count,),
        in_specs=[
            block,
            block,
            pl.BlockSpec((2, heads, tiles, neigh, TILE, HEAD_DIM), lambda c: (0, 0, 0, c + first, 0, 0)),
        ],
        out_specs=[block, block],
        out_shape=[jax.ShapeDtypeStruct(q.shape, BF16)] * 2,
        compiler_params=pltpu.CompilerParams(vmem_limit_bytes=VMEM),
        cost_estimate=pl.CostEstimate(
            flops=128 * rows * width * neigh * tiles * TILE, bytes_accessed=kv.size, transcendentals=0
        ),
        name="attend",
    )(q, g, kv)


def fold_kernel(at_ref, *refs, parts, rows):
    count = (len(refs) - 3) // (1 + parts)
    shares, nears = refs[:count], refs[count : count * (1 + parts)]
    keep_ref, send_ref, block_ref = refs[count * (1 + parts) :]
    blocks = keep_ref.shape[0]
    core = at_ref[1]

    @pl.loop(0, blocks)
    def _(block):
        at = lax.rem(at_ref[0] + block, blocks) * (2 * rows)
        cols = pl.ds(pl.multiple_of(at, 2 * rows), 2 * rows)
        total = jnp.zeros(block_ref.shape, F32)
        for i, share in enumerate(shares):
            low = 0
            for near in nears[i * parts : (i + 1) * parts]:
                high = low + near.shape[0]
                total += lax.dot_general(share[low:high, cols], near[...], BOTH_FIRST, preferred_element_type=F32)
                low = high
        block_ref[...] = total
        keep_ref[block] = block_ref[pl.ds(pl.multiple_of(core * rows, rows), rows)]
        send_ref[block] = block_ref[pl.ds(pl.multiple_of((1 - core) * rows, rows), rows)]


def fold(at, shares, nears, blocks):
    width = nears[0][0].shape[1]
    rows = shares[0].shape[1] // (2 * blocks)
    whole = pl.BlockSpec(memory_space=pltpu.VMEM)
    flat = list(shares) + [a for pair in nears for a in pair]
    tokens = sum(a.shape[0] for a in shares)
    return pl.pallas_call(
        functools.partial(fold_kernel, parts=len(nears[0]), rows=rows),
        in_specs=[pl.BlockSpec(memory_space=pltpu.SMEM)] + [whole] * len(flat),
        out_specs=[whole] * 2,
        out_shape=[jax.ShapeDtypeStruct((blocks, rows, width), F32)] * 2,
        scratch_shapes=[pltpu.VMEM((2 * rows, width), F32)],
        compiler_params=pltpu.CompilerParams(vmem_limit_bytes=VMEM),
        cost_estimate=pl.CostEstimate(
            flops=4 * tokens * blocks * rows * width, bytes_accessed=8 << 20, transcendentals=0
        ),
        name="fold",
    )(at, *flat)


def step(array, axis, by):
    size = lax.axis_size(axis)
    return lax.ppermute(array, axis, [(i, (i + by) % size) for i in range(size)])


def local(inputs, w_query, cache_kv, nb_owner, nb_row, out_grad):
    nx, nz, nc = (lax.axis_size(a) for a in DP)
    ndp, nmp = nx * nz * nc, lax.axis_size("mp")
    mx, mz, mc = (lax.axis_index(a) for a in DP)
    my = lax.axis_index("mp")
    tokens, grad_rows = inputs[0], out_grad[0]
    length, d = tokens.shape
    width = w_query.shape[1]
    heads = width // HEAD_DIM
    db_rows, _, nb_len, _ = cache_kv.shape
    _, stretches, neigh = nb_owner.shape
    requests = stretches * neigh
    tiles = nb_len // TILE
    real = length - LEAD

    message = cut(nb_owner, nb_row, cache_kv)
    held = lax.all_to_all(message, DP, split_axis=0, concat_axis=0, tiled=True)

    block = d // nmp
    fans = [lax.dynamic_slice(w_query, ((my + by) % nmp * block, 0), (block, width)) for by in range(nmp)]
    fans = [step(a, "mp", by) if by else a for by, a in enumerate(fans)]
    held, fans = lax.optimization_barrier((held, fans))

    named = held[:, db_rows, : 2 * stretches, :neigh].astype(jnp.int32)
    ids = named[:, :stretches] * (db_rows + 1) + named[:, stretches:]
    send = pick(ids.reshape(-1), held.reshape(-1, TILE, HEAD_DIM))
    got = lax.all_to_all(
        send.reshape(ndp, requests, TILE, HEAD_DIM), DP, split_axis=0, concat_axis=0, tiled=True
    )

    late, weights, grad_rows, _ = lax.optimization_barrier((tokens, w_query, grad_rows, held))
    block = d // nx
    share = [lax.dynamic_slice(late, (SKIP, (mx + by) % nx * block), (length - SKIP, block)) for by in range(nx)]
    share = [step(a, "x", by) if by else a for by, a in enumerate(share)]

    def shifted(array):
        return jnp.concatenate([array[LEAD:], jnp.zeros((LEAD, array.shape[1]), array.dtype)], 0)

    q = shifted(jnp.dot(late, weights, preferred_element_type=F32).astype(BF16))
    g = shifted(grad_rows)
    got, share, q, g = lax.optimization_barrier((got, share, q, g))

    half = stretches // 2 * STRETCH
    got = got.reshape(2, heads, tiles, requests, TILE, HEAD_DIM)
    out, first = attend(q[:half], g[:half], got, neigh, 0)
    out_late, last = attend(q[half:], g[half:], got, neigh, half // STRETCH)
    cut_at = half - LEAD + SKIP
    first, spill = jnp.concatenate([jnp.zeros((LEAD - SKIP, width), BF16), first[:cut_at]], 0), first[cut_at:]
    last = jnp.concatenate([spill, last[: real - half]], 0)
    early = [step(first, "x", by) if by else first for by in range(nx)]
    last, early[1] = lax.optimization_barrier((last, early[1]))
    nears = [(early[by], step(last, "x", by) if by else last) for by in range(nx)]
    mine, other = fold(jnp.stack([mz, mc]), share, nears, nz)
    mine += step(other, "core", 1)
    dq = jnp.concatenate([first, last], 0)
    groups = jnp.broadcast_to(dq[None], (nmp,) + dq.shape)
    groups = lax.all_to_all(groups, "mp", split_axis=0, concat_axis=0, tiled=True)
    groups, mine = lax.optimization_barrier((groups, mine))
    terms = [step(mine[by], "z", by) if by else mine[by] for by in range(nz)]

    groups, terms[1] = lax.optimization_barrier((groups, terms[1]))
    query_grad = sum(terms)
    part = 0.0
    for by in range(nmp):
        near = lax.dynamic_index_in_dim(groups, (my - by) % nmp, 0, keepdims=False)
        part += lax.dot_general(near, fans[by], BOTH_LAST, preferred_element_type=F32).astype(BF16).astype(F32)
    part = part.astype(BF16)
    attended = jnp.concatenate([jnp.zeros((LEAD, width), BF16), out, out_late[: real - half]], 0)
    input_grad = jnp.concatenate([jnp.zeros((SKIP, d // nmp), BF16), part], 0)
    return attended[None], input_grad[None], query_grad


def solution(mesh):
    fine = Mesh(mesh.devices.reshape(4, 8, 2, 4), ("x", "z", "core", "mp"))
    return jax.shard_map(
        local,
        mesh=fine,
        in_specs=(
            P(DP, None, None),
            P(None, "mp"),
            P(DP, None, None, "mp"),
            P(DP, None, None),
            P(DP, None, None),
            P(DP, None, "mp"),
        ),
        out_specs=(P(DP, None, "mp"), P(DP, None, "mp"), P(DP, "mp")),
        check_vma=False,
    )
```

```python
import functools

import jax
import jax.numpy as jnp
from jax import lax
from jax.experimental import pallas as pl
from jax.experimental.pallas import tpu as pltpu
from jax.sharding import Mesh
from jax.sharding import PartitionSpec as P

HEAD_DIM = 128
STRETCH = 64
LEAD = STRETCH - 1
TILE = 16
SKIP = LEAD // TILE * TILE
DP = ("x", "z", "core")
VMEM = 32 << 20
BF16, F32 = jnp.bfloat16, jnp.float32
BOTH_LAST = (((1,), (1,)), ((), ()))
BOTH_FIRST = (((0,), (0,)), ((), ()))


def cut_kernel(owner_ref, row_ref, cache_ref, out_ref, named_ref):
    rows = cache_ref.shape[0]
    _, stretches, neigh = owner_ref.shape
    named_ref[...] = jnp.zeros_like(named_ref)
    named_ref[:stretches, :neigh] = owner_ref[0].astype(F32)
    named_ref[stretches : 2 * stretches, :neigh] = row_ref[0].astype(F32)
    _, heads, tiles, _, _, _ = out_ref.shape
    for head in range(heads):
        cols = slice(head * HEAD_DIM, (head + 1) * HEAD_DIM)
        for tile in range(tiles):
            out_ref[0, head, tile, :rows] = cache_ref[:, 0, tile * TILE : (tile + 1) * TILE, cols]
            out_ref[0, head, tile, rows] = named_ref[...].astype(BF16)


def cut(nb_owner, nb_row, cache):
    rows, _, nb_len, width = cache.shape
    tiles, heads, parts = nb_len // TILE, width // HEAD_DIM, 2
    named = pl.BlockSpec(nb_owner.shape, lambda a, t: (0, 0, 0))
    return pl.pallas_call(
        cut_kernel,
        grid=(2, parts),
        in_specs=[
            named,
            named,
            pl.BlockSpec((rows, 1, nb_len // parts, width), lambda a, t: (0, a, t, 0)),
        ],
        out_specs=pl.BlockSpec(
            (1, heads, tiles // parts, rows + 1, TILE, HEAD_DIM), lambda a, t: (a, 0, t, 0, 0, 0)
        ),
        out_shape=jax.ShapeDtypeStruct((2, heads, tiles, rows + 1, TILE, HEAD_DIM), BF16),
        scratch_shapes=[pltpu.VMEM((TILE, HEAD_DIM), F32)],
        compiler_params=pltpu.CompilerParams(vmem_limit_bytes=VMEM),
        cost_estimate=pl.CostEstimate(flops=0, bytes_accessed=4 << 20, transcendentals=0),
        name="cut",
    )(nb_owner, nb_row, cache).reshape(-1, rows + 1, TILE, HEAD_DIM)


def pick_kernel(ids_ref, tiles_ref, out_ref, *, slots):
    base = pl.program_id(0) * slots
    for slot in range(slots):
        out_ref[slot] = tiles_ref[ids_ref[base + slot]]


def pick(ids, tiles):
    count, slots = ids.shape[0], 64
    return pl.pallas_call(
        functools.partial(pick_kernel, slots=slots),
        grid_spec=pltpu.PrefetchScalarGridSpec(
            num_scalar_prefetch=1,
            grid=(count // slots,),
            in_specs=[pl.BlockSpec(tiles.shape, lambda s, ids: (0, 0, 0))],
            out_specs=pl.BlockSpec((slots,) + tiles.shape[1:], lambda s, ids: (s, 0, 0)),
        ),
        out_shape=jax.ShapeDtypeStruct((count,) + tiles.shape[1:], tiles.dtype),
        compiler_params=pltpu.CompilerParams(vmem_limit_bytes=VMEM),
        cost_estimate=pl.CostEstimate(flops=0, bytes_accessed=6 << 20, transcendentals=0),
        name="pick",
    )(ids, tiles)


def attend_kernel(q_ref, g_ref, kv_ref, out_ref, dq_ref, *, heads):
    scale = HEAD_DIM ** (-0.5)
    cols = [slice(h * HEAD_DIM, (h + 1) * HEAD_DIM) for h in range(heads)]
    keys = [kv_ref[0, h].reshape(-1, HEAD_DIM) for h in range(heads)]
    values = [kv_ref[1, h].reshape(-1, HEAD_DIM) for h in range(heads)]
    scores = [
        lax.dot_general(q_ref[:, c], k, BOTH_LAST, preferred_element_type=F32)
        for c, k in zip(cols, keys)
    ]
    dprobs = [
        lax.dot_general(g_ref[:, c], v, BOTH_LAST, preferred_element_type=F32)
        for c, v in zip(cols, values)
    ]
    probs, dscores = [], []
    for score, dprob in zip(scores, dprobs):
        score = score * scale
        exps = jnp.exp(score - jnp.max(score, axis=-1, keepdims=True))
        prob = exps * (1.0 / jnp.sum(exps, axis=-1, keepdims=True))
        delta = jnp.sum(dprob * prob, axis=-1, keepdims=True)
        probs.append(prob.astype(BF16))
        dscores.append((prob * (dprob - delta) * scale).astype(BF16))
    for c, k, v, prob, dscore in zip(cols, keys, values, probs, dscores):
        out_ref[:, c] = jnp.dot(prob, v, preferred_element_type=F32).astype(BF16)
        dq_ref[:, c] = jnp.dot(dscore, k, preferred_element_type=F32).astype(BF16)


def attend(q, g, kv, neigh):
    rows, width = q.shape
    count = rows // STRETCH
    _, heads, tiles, slots, _, _ = kv.shape
    block = pl.BlockSpec((STRETCH, width), lambda c: (c, 0))
    return pl.pallas_call(
        functools.partial(attend_kernel, heads=heads),
        grid=(count,),
        in_specs=[
            block,
            block,
            pl.BlockSpec((2, heads, tiles, neigh, TILE, HEAD_DIM), lambda c: (0, 0, 0, c, 0, 0)),
        ],
        out_specs=[block, block],
        out_shape=[jax.ShapeDtypeStruct(q.shape, BF16)] * 2,
        compiler_params=pltpu.CompilerParams(vmem_limit_bytes=VMEM),
        cost_estimate=pl.CostEstimate(
            flops=10 * rows * width * neigh * tiles * TILE, bytes_accessed=kv.size * 2, transcendentals=0
        ),
        name="attend",
    )(q, g, kv)


def step(array, axis, by):
    size = lax.axis_size(axis)
    return lax.ppermute(array, axis, [(i, (i + by) % size) for i in range(size)])


def local(inputs, w_query, cache_kv, nb_owner, nb_row, out_grad):
    nx, nz, nc = (lax.axis_size(a) for a in DP)
    ndp, nmp = nx * nz * nc, lax.axis_size("mp")
    mx, mz, mc = (lax.axis_index(a) for a in DP)
    my = lax.axis_index("mp")
    tokens, grad_rows = inputs[0], out_grad[0]
    length, d = tokens.shape
    width = w_query.shape[1]
    heads = width // HEAD_DIM
    db_rows, _, nb_len, _ = cache_kv.shape
    _, stretches, neigh = nb_owner.shape
    requests = stretches * neigh
    tiles = nb_len // TILE
    real = length - LEAD

    message = cut(nb_owner, nb_row, cache_kv)
    held = lax.all_to_all(message, DP, split_axis=0, concat_axis=0, tiled=True)

    block = d // nmp
    fans = [lax.dynamic_slice(w_query, ((my + by) % nmp * block, 0), (block, width)) for by in range(nmp)]
    fans = [step(a, "mp", by) if by else a for by, a in enumerate(fans)]
    held, fans = lax.optimization_barrier((held, fans))

    named = held[:, db_rows, : 2 * stretches, :neigh].astype(jnp.int32)
    ids = named[:, :stretches] * (db_rows + 1) + named[:, stretches:]
    send = pick(ids.reshape(-1), held.reshape(-1, TILE, HEAD_DIM))
    got = lax.all_to_all(
        send.reshape(ndp, requests, TILE, HEAD_DIM), DP, split_axis=0, concat_axis=0, tiled=True
    )

    late, weights, grad_rows, _ = lax.optimization_barrier((tokens, w_query, grad_rows, held))
    block = d // nx
    share = [lax.dynamic_slice(late, (SKIP, (mx + by) % nx * block), (length - SKIP, block)) for by in range(nx)]
    share = [step(a, "x", by) if by else a for by, a in enumerate(share)]

    def shifted(array):
        return jnp.concatenate([array[LEAD:], jnp.zeros((LEAD, array.shape[1]), array.dtype)], 0)

    q = shifted(jnp.dot(late, weights, preferred_element_type=F32).astype(BF16))
    g = shifted(grad_rows)
    got, share, q, g = lax.optimization_barrier((got, share, q, g))

    out, dq = attend(q, g, got.reshape(2, heads, tiles, requests, TILE, HEAD_DIM), neigh)
    dq = jnp.concatenate([jnp.zeros((LEAD - SKIP, width), BF16), dq[:real]], 0)

    total = 0.0
    for by in sorted(range(nx), key=lambda by: min(by, nx - by)):
        near = step(dq, "x", by) if by else dq
        total += lax.dot_general(share[by], near, BOTH_FIRST, preferred_element_type=F32)
    total = total.reshape(nz, nc, -1, width)
    mine = lax.dynamic_index_in_dim(total, mc, 1, keepdims=False)
    mine += step(lax.dynamic_index_in_dim(total, 1 - mc, 1, keepdims=False), "core", 1)
    groups = jnp.broadcast_to(dq[None], (nmp,) + dq.shape)
    groups = lax.all_to_all(groups, "mp", split_axis=0, concat_axis=0, tiled=True)
    groups, mine = lax.optimization_barrier((groups, mine))
    pairs = mine.reshape(nz // 2, 2, -1, width)
    away = lax.dynamic_index_in_dim(pairs, 1 - mz % 2, 1, keepdims=False)
    mine = lax.dynamic_index_in_dim(pairs, mz % 2, 1, keepdims=False)
    up = lax.ppermute(away[..., : width // 2], "z", [(i, i ^ 1) for i in range(nz)])
    down = lax.ppermute(away[..., width // 2 :], "z", [(i, ((i + 1) ^ 1) - 1) for i in range(1, nz - 1)] + [(0, nz - 1), (nz - 1, 0)])
    groups, up = lax.optimization_barrier((groups, up))
    mine += jnp.concatenate([up, down], -1)
    terms = [lax.dynamic_index_in_dim(mine, (mz // 2 + by) % (nz // 2), 0, keepdims=False) for by in range(nz // 2)]
    query_grad = sum(step(a, "z", 2 * by) if by else a for by, a in enumerate(terms))
    part = 0.0
    for by in range(nmp):
        near = lax.dynamic_index_in_dim(groups, (my - by) % nmp, 0, keepdims=False)
        part += lax.dot_general(near, fans[by], BOTH_LAST, preferred_element_type=F32).astype(BF16).astype(F32)
    part = part.astype(BF16)
    attended = jnp.concatenate([jnp.zeros((LEAD, width), BF16), out[:real]], 0)
    input_grad = jnp.concatenate([jnp.zeros((SKIP, d // nmp), BF16), part], 0)
    return attended[None], input_grad[None], query_grad


def solution(mesh):
    fine = Mesh(mesh.devices.reshape(4, 8, 2, 4), ("x", "z", "core", "mp"))
    return jax.shard_map(
        local,
        mesh=fine,
        in_specs=(
            P(DP, None, None),
            P(None, "mp"),
            P(DP, None, None, "mp"),
            P(DP, None, None),
            P(DP, None, None),
            P(DP, None, "mp"),
        ),
        out_specs=(P(DP, None, "mp"), P(DP, None, "mp"), P(DP, "mp")),
        check_vma=False,
    )
```

```python
import functools

import jax
import jax.numpy as jnp
from jax import lax
from jax.experimental import pallas as pl
from jax.experimental.pallas import tpu as pltpu
from jax.sharding import Mesh
from jax.sharding import PartitionSpec as P

HEAD_DIM = 128
STRETCH = 64
LEAD = STRETCH - 1
TILE = 16
SKIP = LEAD // TILE * TILE
DP = ("x", "z", "core")
VMEM = 32 << 20
BF16, F32 = jnp.bfloat16, jnp.float32
BOTH_LAST = (((1,), (1,)), ((), ()))
BOTH_FIRST = (((0,), (0,)), ((), ()))


def cut_kernel(named_ref, cache_ref, out_ref):
    rows = cache_ref.shape[0]
    _, heads, tiles, _, _, _ = out_ref.shape
    for head in range(heads):
        cols = slice(head * HEAD_DIM, (head + 1) * HEAD_DIM)
        for tile in range(tiles):
            out_ref[0, head, tile, :rows] = cache_ref[:, 0, tile * TILE : (tile + 1) * TILE, cols]
            out_ref[0, head, tile, rows] = named_ref[...]


def cut(named, cache):
    rows, _, nb_len, width = cache.shape
    tiles, heads = nb_len // TILE, width // HEAD_DIM
    return pl.pallas_call(
        cut_kernel,
        grid=(2,),
        in_specs=[
            pl.BlockSpec(named.shape, lambda a: (0, 0)),
            pl.BlockSpec((rows, 1, nb_len, width), lambda a: (0, a, 0, 0)),
        ],
        out_specs=pl.BlockSpec((1, heads, tiles, rows + 1, TILE, HEAD_DIM), lambda a: (a, 0, 0, 0, 0, 0)),
        out_shape=jax.ShapeDtypeStruct((2, heads, tiles, rows + 1, TILE, HEAD_DIM), BF16),
        compiler_params=pltpu.CompilerParams(vmem_limit_bytes=60 << 20),
        cost_estimate=pl.CostEstimate(flops=0, bytes_accessed=4 << 20, transcendentals=0),
        name="cut",
    )(named, cache).reshape(-1, rows + 1, TILE, HEAD_DIM)


def pick_kernel(ids_ref, tiles_ref, out_ref, *, slots):
    base = pl.program_id(0) * slots
    for slot in range(slots):
        out_ref[slot] = tiles_ref[ids_ref[base + slot]]


def pick(ids, tiles):
    count, slots = ids.shape[0], 64
    return pl.pallas_call(
        functools.partial(pick_kernel, slots=slots),
        grid_spec=pltpu.PrefetchScalarGridSpec(
            num_scalar_prefetch=1,
            grid=(count // slots,),
            in_specs=[pl.BlockSpec(tiles.shape, lambda s, ids: (0, 0, 0))],
            out_specs=pl.BlockSpec((slots,) + tiles.shape[1:], lambda s, ids: (s, 0, 0)),
        ),
        out_shape=jax.ShapeDtypeStruct((count,) + tiles.shape[1:], tiles.dtype),
        compiler_params=pltpu.CompilerParams(vmem_limit_bytes=VMEM),
        cost_estimate=pl.CostEstimate(flops=0, bytes_accessed=6 << 20, transcendentals=0),
        name="pick",
    )(ids, tiles)


def attend_kernel(q_ref, g_ref, kv_ref, out_ref, dq_ref, *, heads):
    for i in range(q_ref.shape[0] // STRETCH):
        rows = pl.ds(i * STRETCH, STRETCH)
        kv = kv_ref.at[:, :, :, :, i]
        attend_stretch(q_ref.at[rows], g_ref.at[rows], kv, out_ref.at[rows], dq_ref.at[rows], heads)


def attend_stretch(q_ref, g_ref, kv_ref, out_ref, dq_ref, heads):
    scale = HEAD_DIM ** (-0.5)
    cols = [slice(h * HEAD_DIM, (h + 1) * HEAD_DIM) for h in range(heads)]
    keys = [kv_ref[0, h].reshape(-1, HEAD_DIM) for h in range(heads)]
    values = [kv_ref[1, h].reshape(-1, HEAD_DIM) for h in range(heads)]
    scores = [
        lax.dot_general(q_ref[:, c], k, BOTH_LAST, preferred_element_type=F32)
        for c, k in zip(cols, keys)
    ]
    dprobs = [
        lax.dot_general(g_ref[:, c], v, BOTH_LAST, preferred_element_type=F32)
        for c, v in zip(cols, values)
    ]
    probs, dscores = [], []
    for score, dprob in zip(scores, dprobs):
        score = score * scale
        exps = jnp.exp(score - jnp.max(score, axis=-1, keepdims=True))
        prob = exps * (1.0 / jnp.sum(exps, axis=-1, keepdims=True))
        delta = jnp.sum(dprob * prob, axis=-1, keepdims=True)
        probs.append(prob.astype(BF16))
        dscores.append((prob * (dprob - delta) * scale).astype(BF16))
    for c, k, v, prob, dscore in zip(cols, keys, values, probs, dscores):
        out_ref[:, c] = jnp.dot(prob, v, preferred_element_type=F32).astype(BF16)
        dq_ref[:, c] = jnp.dot(dscore, k, preferred_element_type=F32).astype(BF16)


def attend(q, g, kv):
    rows, width = q.shape
    count, together = rows // STRETCH, 2
    _, heads, tiles, neigh, _, _, _ = kv.shape
    block = pl.BlockSpec((together * STRETCH, width), lambda c: (c, 0))
    return pl.pallas_call(
        functools.partial(attend_kernel, heads=heads),
        grid=(count // together,),
        in_specs=[
            block,
            block,
            pl.BlockSpec(
                (2, heads, tiles, neigh, together, TILE, HEAD_DIM), lambda c: (0, 0, 0, 0, c, 0, 0)
            ),
        ],
        out_specs=[block, block],
        out_shape=[jax.ShapeDtypeStruct(q.shape, BF16)] * 2,
        compiler_params=pltpu.CompilerParams(vmem_limit_bytes=VMEM),
        cost_estimate=pl.CostEstimate(
            flops=10 * rows * width * neigh * tiles * TILE, bytes_accessed=kv.size * 2, transcendentals=0
        ),
        name="attend",
    )(q, g, kv)


def step(array, axis, by):
    size = lax.axis_size(axis)
    return lax.ppermute(array, axis, [(i, (i + by) % size) for i in range(size)])


def local(inputs, w_query, cache_kv, nb_owner, nb_row, out_grad):
    nx, nz, nc = (lax.axis_size(a) for a in DP)
    ndp, nmp = nx * nz * nc, lax.axis_size("mp")
    mx, mz, mc = (lax.axis_index(a) for a in DP)
    my = lax.axis_index("mp")
    tokens, grad_rows = inputs[0], out_grad[0]
    length, d = tokens.shape
    width = w_query.shape[1]
    heads = width // HEAD_DIM
    db_rows, _, nb_len, _ = cache_kv.shape
    _, stretches, neigh = nb_owner.shape
    requests = stretches * neigh
    tiles = nb_len // TILE
    real = length - LEAD

    lanes = (0, HEAD_DIM - stretches)
    named = jnp.pad(nb_owner[0].T, ((0, TILE - neigh), lanes)) + jnp.pad(nb_row[0].T, ((neigh, TILE - 2 * neigh), lanes))
    message = cut(named.astype(BF16), cache_kv)
    held = lax.all_to_all(message, DP, split_axis=0, concat_axis=0, tiled=True)

    block = d // nmp
    fans = [lax.dynamic_slice(w_query, ((my + by) % nmp * block, 0), (block, width)) for by in range(nmp)]
    fans = [step(a, "mp", by) if by else a for by, a in enumerate(fans)]
    held, fans = lax.optimization_barrier((held, fans))

    named = held[:, db_rows, : 2 * neigh, :stretches].astype(jnp.int32)
    ids = named[:, :neigh] * (db_rows + 1) + named[:, neigh:]
    send = pick(ids.reshape(-1), held.reshape(-1, TILE, HEAD_DIM))
    got = lax.all_to_all(
        send.reshape(ndp, requests, TILE, HEAD_DIM), DP, split_axis=0, concat_axis=0, tiled=True
    )

    late, weights, grad_rows, _ = lax.optimization_barrier((tokens, w_query, grad_rows, held))
    block = d // nx
    share = [lax.dynamic_slice(late, (SKIP, (mx + by) % nx * block), (length - SKIP, block)) for by in range(nx)]
    share = [step(a, "x", by) if by else a for by, a in enumerate(share)]

    def shifted(array):
        return jnp.concatenate([array[LEAD:], jnp.zeros((LEAD, array.shape[1]), array.dtype)], 0)

    q = shifted(jnp.dot(late, weights, preferred_element_type=F32).astype(BF16))
    g = shifted(grad_rows)
    got, share, q, g = lax.optimization_barrier((got, share, q, g))

    out, dq = attend(q, g, got.reshape(2, heads, tiles, neigh, stretches, TILE, HEAD_DIM))
    dq = jnp.concatenate([jnp.zeros((LEAD - SKIP, width), BF16), dq[:real]], 0)

    total = 0.0
    for by in sorted(range(nx), key=lambda by: min(by, nx - by)):
        near = step(dq, "x", by) if by else dq
        if 2 * by == nx:
            own = lax.dot_general(dq, fans[0], BOTH_LAST, preferred_element_type=F32).astype(BF16)
            near, own = lax.optimization_barrier((near, own))
        total += lax.dot_general(share[by], near, BOTH_FIRST, preferred_element_type=F32)
    total = total.reshape(nz, nc, -1, width)
    mine = lax.dynamic_index_in_dim(total, mc, 1, keepdims=False)
    mine += step(lax.dynamic_index_in_dim(total, 1 - mc, 1, keepdims=False), "core", 1)
    groups = jnp.broadcast_to(dq[None], (nmp,) + dq.shape)
    groups = lax.all_to_all(groups, "mp", split_axis=0, concat_axis=0, tiled=True)
    groups, mine = lax.optimization_barrier((groups, mine))
    pairs = mine.reshape(nz // 2, 2, -1, width)
    away = lax.dynamic_index_in_dim(pairs, 1 - mz % 2, 1, keepdims=False)
    mine = lax.dynamic_index_in_dim(pairs, mz % 2, 1, keepdims=False)
    up = lax.ppermute(away[..., : width // 2], "z", [(i, i ^ 1) for i in range(nz)])
    down = lax.ppermute(away[..., width // 2 :], "z", [(i, ((i + 1) ^ 1) - 1) for i in range(1, nz - 1)] + [(0, nz - 1), (nz - 1, 0)])
    parts = [own]
    for by in range(1, nmp):
        if by == nmp - 1:
            up, parts, groups = lax.optimization_barrier((up, parts, groups))
        near = lax.dynamic_index_in_dim(groups, (my - by) % nmp, 0, keepdims=False)
        parts.append(lax.dot_general(near, fans[by], BOTH_LAST, preferred_element_type=F32).astype(BF16))
    mine += jnp.concatenate([up, down], -1)
    terms = [lax.dynamic_index_in_dim(mine, (mz // 2 + by) % (nz // 2), 0, keepdims=False) for by in range(nz // 2)]
    query_grad = sum(step(a, "z", 2 * by) if by else a for by, a in enumerate(terms))
    part = sum(a.astype(F32) for a in parts).astype(BF16)
    attended = jnp.concatenate([jnp.zeros((LEAD, width), BF16), out[:real]], 0)
    input_grad = jnp.concatenate([jnp.zeros((SKIP, d // nmp), BF16), part], 0)
    return attended[None], input_grad[None], query_grad


def solution(mesh):
    fine = Mesh(mesh.devices.reshape(4, 8, 2, 4), ("x", "z", "core", "mp"))
    return jax.shard_map(
        local,
        mesh=fine,
        in_specs=(
            P(DP, None, None),
            P(None, "mp"),
            P(DP, None, None, "mp"),
            P(DP, None, None),
            P(DP, None, None),
            P(DP, None, "mp"),
        ),
        out_specs=(P(DP, None, "mp"), P(DP, None, "mp"), P(DP, "mp")),
        check_vma=False,
    )
```

```python
import functools

import jax
import jax.numpy as jnp
from jax import lax
from jax.experimental import pallas as pl
from jax.experimental.pallas import tpu as pltpu
from jax.sharding import Mesh
from jax.sharding import PartitionSpec as P

HEAD_DIM = 128
STRETCH = 64
LEAD = STRETCH - 1
TILE = 16
SKIP = LEAD // TILE * TILE
DP = ("x", "z", "core")
VMEM = 32 << 20
BF16, F32 = jnp.bfloat16, jnp.float32
BOTH_LAST = (((1,), (1,)), ((), ()))
BOTH_FIRST = (((0,), (0,)), ((), ()))


def cut_kernel(named_ref, cache_ref, out_ref):
    rows = cache_ref.shape[0]
    _, heads, tiles, _, _, _ = out_ref.shape
    for head in range(heads):
        cols = slice(head * HEAD_DIM, (head + 1) * HEAD_DIM)
        for tile in range(tiles):
            out_ref[0, head, tile, :rows] = cache_ref[:, 0, tile * TILE : (tile + 1) * TILE, cols]
            out_ref[0, head, tile, rows] = named_ref[...]


def cut(named, cache):
    rows, _, nb_len, width = cache.shape
    tiles, heads = nb_len // TILE, width // HEAD_DIM
    return pl.pallas_call(
        cut_kernel,
        grid=(2,),
        in_specs=[
            pl.BlockSpec(named.shape, lambda a: (0, 0)),
            pl.BlockSpec((rows, 1, nb_len, width), lambda a: (0, a, 0, 0)),
        ],
        out_specs=pl.BlockSpec((1, heads, tiles, rows + 1, TILE, HEAD_DIM), lambda a: (a, 0, 0, 0, 0, 0)),
        out_shape=jax.ShapeDtypeStruct((2, heads, tiles, rows + 1, TILE, HEAD_DIM), BF16),
        compiler_params=pltpu.CompilerParams(vmem_limit_bytes=60 << 20),
        cost_estimate=pl.CostEstimate(flops=0, bytes_accessed=4 << 20, transcendentals=0),
        name="cut",
    )(named, cache).reshape(-1, rows + 1, TILE, HEAD_DIM)


def pick_kernel(ids_ref, tiles_ref, out_ref, *, slots):
    base = pl.program_id(0) * slots
    for slot in range(slots):
        out_ref[slot] = tiles_ref[ids_ref[base + slot]]


def pick(ids, tiles):
    count, slots = ids.shape[0], 64
    return pl.pallas_call(
        functools.partial(pick_kernel, slots=slots),
        grid_spec=pltpu.PrefetchScalarGridSpec(
            num_scalar_prefetch=1,
            grid=(count // slots,),
            in_specs=[pl.BlockSpec(tiles.shape, lambda s, ids: (0, 0, 0))],
            out_specs=pl.BlockSpec((slots,) + tiles.shape[1:], lambda s, ids: (s, 0, 0)),
        ),
        out_shape=jax.ShapeDtypeStruct((count,) + tiles.shape[1:], tiles.dtype),
        compiler_params=pltpu.CompilerParams(vmem_limit_bytes=VMEM),
        cost_estimate=pl.CostEstimate(flops=0, bytes_accessed=6 << 20, transcendentals=0),
        name="pick",
    )(ids, tiles)


def attend_kernel(q_ref, g_ref, kv_ref, out_ref, dq_ref, *, heads):
    for i in range(q_ref.shape[0] // STRETCH):
        rows = pl.ds(i * STRETCH, STRETCH)
        kv = kv_ref.at[:, :, :, :, i]
        attend_stretch(q_ref.at[rows], g_ref.at[rows], kv, out_ref.at[rows], dq_ref.at[rows], heads)


def attend_stretch(q_ref, g_ref, kv_ref, out_ref, dq_ref, heads):
    scale = HEAD_DIM ** (-0.5)
    cols = [slice(h * HEAD_DIM, (h + 1) * HEAD_DIM) for h in range(heads)]
    keys = [kv_ref[0, h].reshape(-1, HEAD_DIM) for h in range(heads)]
    values = [kv_ref[1, h].reshape(-1, HEAD_DIM) for h in range(heads)]
    scores = [
        lax.dot_general(q_ref[:, c], k, BOTH_LAST, preferred_element_type=F32)
        for c, k in zip(cols, keys)
    ]
    dprobs = [
        lax.dot_general(g_ref[:, c], v, BOTH_LAST, preferred_element_type=F32)
        for c, v in zip(cols, values)
    ]
    probs, dscores = [], []
    for score, dprob in zip(scores, dprobs):
        score = score * scale
        exps = jnp.exp(score - jnp.max(score, axis=-1, keepdims=True))
        prob = exps * (1.0 / jnp.sum(exps, axis=-1, keepdims=True))
        delta = jnp.sum(dprob * prob, axis=-1, keepdims=True)
        probs.append(prob.astype(BF16))
        dscores.append((prob * (dprob - delta) * scale).astype(BF16))
    for c, k, v, prob, dscore in zip(cols, keys, values, probs, dscores):
        out_ref[:, c] = jnp.dot(prob, v, preferred_element_type=F32).astype(BF16)
        dq_ref[:, c] = jnp.dot(dscore, k, preferred_element_type=F32).astype(BF16)


def attend(q, g, kv):
    rows, width = q.shape
    count, together = rows // STRETCH, 2
    _, heads, tiles, neigh, _, _, _ = kv.shape
    block = pl.BlockSpec((together * STRETCH, width), lambda c: (c, 0))
    return pl.pallas_call(
        functools.partial(attend_kernel, heads=heads),
        grid=(count // together,),
        in_specs=[
            block,
            block,
            pl.BlockSpec(
                (2, heads, tiles, neigh, together, TILE, HEAD_DIM), lambda c: (0, 0, 0, 0, c, 0, 0)
            ),
        ],
        out_specs=[block, block],
        out_shape=[jax.ShapeDtypeStruct(q.shape, BF16)] * 2,
        compiler_params=pltpu.CompilerParams(vmem_limit_bytes=VMEM),
        cost_estimate=pl.CostEstimate(
            flops=10 * rows * width * neigh * tiles * TILE, bytes_accessed=kv.size * 2, transcendentals=0
        ),
        name="attend",
    )(q, g, kv)


def split_kernel(core_ref, share_ref, own_ref, other_ref, *, rows):
    lane = lax.broadcasted_iota(jnp.int32, (share_ref.shape[0], 2 * rows), 1)
    first = core_ref[0] == 0
    for i in range(own_ref.shape[1] // (2 * rows)):
        even = share_ref[:, 4 * i * rows : (4 * i + 2) * rows].astype(F32)
        odd = share_ref[:, (4 * i + 2) * rows : (4 * i + 4) * rows].astype(F32)
        low = jnp.where(lane < rows, even, pltpu.roll(odd, rows, 1)).astype(BF16)
        high = jnp.where(lane < rows, pltpu.roll(even, rows, 1), odd).astype(BF16)
        own_ref[:, 2 * i * rows : 2 * (i + 1) * rows] = jnp.where(first, low, high)
        other_ref[:, 2 * i * rows : 2 * (i + 1) * rows] = jnp.where(first, high, low)


def split(core, share, rows):
    tokens, columns = share.shape
    whole = pl.BlockSpec((tokens, columns // 2), lambda: (0, 0))
    return pl.pallas_call(
        functools.partial(split_kernel, rows=rows),
        in_specs=[pl.BlockSpec(memory_space=pltpu.SMEM), pl.BlockSpec((tokens, columns), lambda: (0, 0))],
        out_specs=[whole] * 2,
        out_shape=[jax.ShapeDtypeStruct((tokens, columns // 2), BF16)] * 2,
        compiler_params=pltpu.CompilerParams(vmem_limit_bytes=16 << 20),
        cost_estimate=pl.CostEstimate(flops=0, bytes_accessed=4 << 20, transcendentals=0),
        name="split",
    )(core.reshape(1), share)


def step(array, axis, by):
    size = lax.axis_size(axis)
    return lax.ppermute(array, axis, [(i, (i + by) % size) for i in range(size)])


def local(inputs, w_query, cache_kv, nb_owner, nb_row, out_grad):
    nx, nz, nc = (lax.axis_size(a) for a in DP)
    ndp, nmp = nx * nz * nc, lax.axis_size("mp")
    mx, mz, mc = (lax.axis_index(a) for a in DP)
    my = lax.axis_index("mp")
    tokens, grad_rows = inputs[0], out_grad[0]
    length, d = tokens.shape
    width = w_query.shape[1]
    heads = width // HEAD_DIM
    db_rows, _, nb_len, _ = cache_kv.shape
    _, stretches, neigh = nb_owner.shape
    requests = stretches * neigh
    tiles = nb_len // TILE
    real = length - LEAD

    lanes = (0, HEAD_DIM - stretches)
    named = jnp.pad(nb_owner[0].T, ((0, TILE - neigh), lanes)) + jnp.pad(nb_row[0].T, ((neigh, TILE - 2 * neigh), lanes))
    message = cut(named.astype(BF16), cache_kv)
    held = lax.all_to_all(message, DP, split_axis=0, concat_axis=0, tiled=True)

    block = d // nmp
    fans = [lax.dynamic_slice(w_query, ((my + by) % nmp * block, 0), (block, width)) for by in range(nmp)]
    fans = [step(a, "mp", by) if by else a for by, a in enumerate(fans)]
    held, fans = lax.optimization_barrier((held, fans))

    named = held[:, db_rows, : 2 * neigh, :stretches].astype(jnp.int32)
    ids = named[:, :neigh] * (db_rows + 1) + named[:, neigh:]
    send = pick(ids.reshape(-1), held.reshape(-1, TILE, HEAD_DIM))
    got = lax.all_to_all(
        send.reshape(ndp, requests, TILE, HEAD_DIM), DP, split_axis=0, concat_axis=0, tiled=True
    )

    late, weights, grad_rows, _ = lax.optimization_barrier((tokens, w_query, grad_rows, held))
    block = d // nx
    share = [lax.dynamic_slice(late, (SKIP, (mx + by) % nx * block), (length - SKIP, block)) for by in range(nx)]
    share = [split(mc, step(a, "x", by) if by else a, d // ndp) for by, a in enumerate(share)]

    def shifted(array):
        return jnp.concatenate([array[LEAD:], jnp.zeros((LEAD, array.shape[1]), array.dtype)], 0)

    q = shifted(jnp.dot(late, weights, preferred_element_type=F32).astype(BF16))
    g = shifted(grad_rows)
    got, share, q, g = lax.optimization_barrier((got, share, q, g))

    out, dq = attend(q, g, got.reshape(2, heads, tiles, neigh, stretches, TILE, HEAD_DIM))
    dq = jnp.concatenate([jnp.zeros((LEAD - SKIP, width), BF16), dq[:real]], 0)

    mine = other = 0.0
    order = sorted(range(nx), key=lambda by: min(by, nx - by))
    for by in order:
        near = step(dq, "x", by) if by else dq
        if by == 1:
            own = lax.dot_general(dq, fans[0], BOTH_LAST, preferred_element_type=F32).astype(BF16)
            near, own = lax.optimization_barrier((near, own))
        if by == order[-1]:
            near, mine, other = lax.optimization_barrier((near, mine, other))
        other += lax.dot_general(share[by][1], near, BOTH_FIRST, preferred_element_type=F32)
        mine += lax.dot_general(share[by][0], near, BOTH_FIRST, preferred_element_type=F32)
    mine += step(other, "core", 1)
    groups = jnp.broadcast_to(dq[None], (nmp,) + dq.shape)
    groups = lax.all_to_all(groups, "mp", split_axis=0, concat_axis=0, tiled=True)
    groups, mine = lax.optimization_barrier((groups, mine))
    pairs = mine.reshape(nz // 2, 2, -1, width)
    away = lax.dynamic_index_in_dim(pairs, 1 - mz % 2, 1, keepdims=False)
    mine = lax.dynamic_index_in_dim(pairs, mz % 2, 1, keepdims=False)
    up = lax.ppermute(away[..., : width // 2], "z", [(i, i ^ 1) for i in range(nz)])
    down = lax.ppermute(away[..., width // 2 :], "z", [(i, ((i + 1) ^ 1) - 1) for i in range(1, nz - 1)] + [(0, nz - 1), (nz - 1, 0)])
    parts = [own]
    for by in range(1, nmp):
        if by == nmp - 1:
            up, parts, groups = lax.optimization_barrier((up, parts, groups))
        near = lax.dynamic_index_in_dim(groups, (my - by) % nmp, 0, keepdims=False)
        parts.append(lax.dot_general(near, fans[by], BOTH_LAST, preferred_element_type=F32).astype(BF16))
    mine += jnp.concatenate([up, down], -1)
    terms = [lax.dynamic_index_in_dim(mine, (mz // 2 + by) % (nz // 2), 0, keepdims=False) for by in range(nz // 2)]
    query_grad = sum(step(a, "z", 2 * by) if by else a for by, a in enumerate(terms))
    part = sum(a.astype(F32) for a in parts).astype(BF16)
    attended = jnp.concatenate([jnp.zeros((LEAD, width), BF16), out[:real]], 0)
    input_grad = jnp.concatenate([jnp.zeros((SKIP, d // nmp), BF16), part], 0)
    return attended[None], input_grad[None], query_grad


def solution(mesh):
    fine = Mesh(mesh.devices.reshape(4, 8, 2, 4), ("x", "z", "core", "mp"))
    return jax.shard_map(
        local,
        mesh=fine,
        in_specs=(
            P(DP, None, None),
            P(None, "mp"),
            P(DP, None, None, "mp"),
            P(DP, None, None),
            P(DP, None, None),
            P(DP, None, "mp"),
        ),
        out_specs=(P(DP, None, "mp"), P(DP, None, "mp"), P(DP, "mp")),
        check_vma=False,
    )
```

```python
import functools

import jax
import jax.numpy as jnp
from jax import lax
from jax.experimental import pallas as pl
from jax.experimental.pallas import tpu as pltpu
from jax.sharding import Mesh
from jax.sharding import PartitionSpec as P

HEAD_DIM = 128
STRETCH = 64
LEAD = STRETCH - 1
TILE = 16
SKIP = LEAD // TILE * TILE
DP = ("x", "z", "core")
VMEM = 32 << 20
BF16, F32 = jnp.bfloat16, jnp.float32
BOTH_LAST = (((1,), (1,)), ((), ()))
BOTH_FIRST = (((0,), (0,)), ((), ()))


def cut_kernel(named_ref, cache_ref, out_ref):
    rows = cache_ref.shape[0]
    _, heads, tiles, _, _, _ = out_ref.shape
    for head in range(heads):
        cols = slice(head * HEAD_DIM, (head + 1) * HEAD_DIM)
        for tile in range(tiles):
            out_ref[0, head, tile, :rows] = cache_ref[:, 0, tile * TILE : (tile + 1) * TILE, cols]
            out_ref[0, head, tile, rows] = named_ref[...]


def cut(named, cache):
    rows, _, nb_len, width = cache.shape
    tiles, heads = nb_len // TILE, width // HEAD_DIM
    return pl.pallas_call(
        cut_kernel,
        grid=(2,),
        in_specs=[
            pl.BlockSpec(named.shape, lambda a: (0, 0)),
            pl.BlockSpec((rows, 1, nb_len, width), lambda a: (0, a, 0, 0)),
        ],
        out_specs=pl.BlockSpec((1, heads, tiles, rows + 1, TILE, HEAD_DIM), lambda a: (a, 0, 0, 0, 0, 0)),
        out_shape=jax.ShapeDtypeStruct((2, heads, tiles, rows + 1, TILE, HEAD_DIM), BF16),
        compiler_params=pltpu.CompilerParams(vmem_limit_bytes=60 << 20),
        cost_estimate=pl.CostEstimate(flops=0, bytes_accessed=4 << 20, transcendentals=0),
        name="cut",
    )(named, cache).reshape(-1, rows + 1, TILE, HEAD_DIM)


def pick_kernel(ids_ref, tiles_ref, out_ref, *, slots):
    base = pl.program_id(0) * slots
    for slot in range(slots):
        out_ref[slot] = tiles_ref[ids_ref[base + slot]]


def pick(ids, tiles):
    count, slots = ids.shape[0], 64
    return pl.pallas_call(
        functools.partial(pick_kernel, slots=slots),
        grid_spec=pltpu.PrefetchScalarGridSpec(
            num_scalar_prefetch=1,
            grid=(count // slots,),
            in_specs=[pl.BlockSpec(tiles.shape, lambda s, ids: (0, 0, 0))],
            out_specs=pl.BlockSpec((slots,) + tiles.shape[1:], lambda s, ids: (s, 0, 0)),
        ),
        out_shape=jax.ShapeDtypeStruct((count,) + tiles.shape[1:], tiles.dtype),
        compiler_params=pltpu.CompilerParams(vmem_limit_bytes=VMEM),
        cost_estimate=pl.CostEstimate(flops=0, bytes_accessed=6 << 20, transcendentals=0),
        name="pick",
    )(ids, tiles)


def attend_kernel(q_ref, g_ref, kv_ref, out_ref, dq_ref, *, heads):
    for i in range(q_ref.shape[0] // STRETCH):
        rows = pl.ds(i * STRETCH, STRETCH)
        kv = kv_ref.at[:, :, :, :, i]
        attend_stretch(q_ref.at[rows], g_ref.at[rows], kv, out_ref.at[rows], dq_ref.at[rows], heads)


def attend_stretch(q_ref, g_ref, kv_ref, out_ref, dq_ref, heads):
    scale = HEAD_DIM ** (-0.5)
    cols = [slice(h * HEAD_DIM, (h + 1) * HEAD_DIM) for h in range(heads)]
    keys = [kv_ref[0, h].reshape(-1, HEAD_DIM) for h in range(heads)]
    values = [kv_ref[1, h].reshape(-1, HEAD_DIM) for h in range(heads)]
    scores = [
        lax.dot_general(q_ref[:, c], k, BOTH_LAST, preferred_element_type=F32)
        for c, k in zip(cols, keys)
    ]
    dprobs = [
        lax.dot_general(g_ref[:, c], v, BOTH_LAST, preferred_element_type=F32)
        for c, v in zip(cols, values)
    ]
    probs, dscores = [], []
    for score, dprob in zip(scores, dprobs):
        score = score * scale
        exps = jnp.exp(score - jnp.max(score, axis=-1, keepdims=True))
        prob = exps * (1.0 / jnp.sum(exps, axis=-1, keepdims=True))
        delta = jnp.sum(dprob * prob, axis=-1, keepdims=True)
        probs.append(prob.astype(BF16))
        dscores.append((prob * (dprob - delta) * scale).astype(BF16))
    for c, k, v, prob, dscore in zip(cols, keys, values, probs, dscores):
        out_ref[:, c] = jnp.dot(prob, v, preferred_element_type=F32).astype(BF16)
        dq_ref[:, c] = jnp.dot(dscore, k, preferred_element_type=F32).astype(BF16)


def attend(q, g, kv):
    rows, width = q.shape
    count, together = rows // STRETCH, 2
    _, heads, tiles, neigh, _, _, _ = kv.shape
    block = pl.BlockSpec((together * STRETCH, width), lambda c: (c, 0))
    return pl.pallas_call(
        functools.partial(attend_kernel, heads=heads),
        grid=(count // together,),
        in_specs=[
            block,
            block,
            pl.BlockSpec(
                (2, heads, tiles, neigh, together, TILE, HEAD_DIM), lambda c: (0, 0, 0, 0, c, 0, 0)
            ),
        ],
        out_specs=[block, block],
        out_shape=[jax.ShapeDtypeStruct(q.shape, BF16)] * 2,
        compiler_params=pltpu.CompilerParams(vmem_limit_bytes=VMEM),
        cost_estimate=pl.CostEstimate(
            flops=10 * rows * width * neigh * tiles * TILE, bytes_accessed=kv.size * 2, transcendentals=0
        ),
        name="attend",
    )(q, g, kv)


def split_kernel(core_ref, share_ref, own_ref, other_ref, *, rows):
    lane = lax.broadcasted_iota(jnp.int32, (share_ref.shape[0], 2 * rows), 1)
    first = core_ref[0] == 0
    for i in range(own_ref.shape[1] // (2 * rows)):
        even = share_ref[:, 4 * i * rows : (4 * i + 2) * rows].astype(F32)
        odd = share_ref[:, (4 * i + 2) * rows : (4 * i + 4) * rows].astype(F32)
        low = jnp.where(lane < rows, even, pltpu.roll(odd, rows, 1)).astype(BF16)
        high = jnp.where(lane < rows, pltpu.roll(even, rows, 1), odd).astype(BF16)
        own_ref[:, 2 * i * rows : 2 * (i + 1) * rows] = jnp.where(first, low, high)
        other_ref[:, 2 * i * rows : 2 * (i + 1) * rows] = jnp.where(first, high, low)


def split(core, share, rows):
    tokens, columns = share.shape
    whole = pl.BlockSpec((tokens, columns // 2), lambda: (0, 0))
    return pl.pallas_call(
        functools.partial(split_kernel, rows=rows),
        in_specs=[pl.BlockSpec(memory_space=pltpu.SMEM), pl.BlockSpec((tokens, columns), lambda: (0, 0))],
        out_specs=[whole] * 2,
        out_shape=[jax.ShapeDtypeStruct((tokens, columns // 2), BF16)] * 2,
        compiler_params=pltpu.CompilerParams(vmem_limit_bytes=16 << 20),
        cost_estimate=pl.CostEstimate(flops=0, bytes_accessed=4 << 20, transcendentals=0),
        name="split",
    )(core.reshape(1), share)


def step(array, axis, by):
    size = lax.axis_size(axis)
    return lax.ppermute(array, axis, [(i, (i + by) % size) for i in range(size)])


def local(inputs, w_query, cache_kv, nb_owner, nb_row, out_grad):
    nx, nz, nc = (lax.axis_size(a) for a in DP)
    ndp, nmp = nx * nz * nc, lax.axis_size("mp")
    mx, mz, mc = (lax.axis_index(a) for a in DP)
    my = lax.axis_index("mp")
    tokens, grad_rows = inputs[0], out_grad[0]
    length, d = tokens.shape
    width = w_query.shape[1]
    heads = width // HEAD_DIM
    db_rows, _, nb_len, _ = cache_kv.shape
    _, stretches, neigh = nb_owner.shape
    requests = stretches * neigh
    tiles = nb_len // TILE
    real = length - LEAD

    lanes = (0, HEAD_DIM - stretches)
    named = jnp.pad(nb_owner[0].T, ((0, TILE - neigh), lanes)) + jnp.pad(nb_row[0].T, ((neigh, TILE - 2 * neigh), lanes))
    message = cut(named.astype(BF16), cache_kv)
    held = lax.all_to_all(message, DP, split_axis=0, concat_axis=0, tiled=True)

    block = d // nmp
    fans = [lax.dynamic_slice(w_query, ((my + by) % nmp * block, 0), (block, width)) for by in range(nmp)]
    fans = [step(a, "mp", by) if by else a for by, a in enumerate(fans)]
    held, fans = lax.optimization_barrier((held, fans))

    named = held[:, db_rows, : 2 * neigh, :stretches].astype(jnp.int32)
    ids = named[:, :neigh] * (db_rows + 1) + named[:, neigh:]
    send = pick(ids.reshape(-1), held.reshape(-1, TILE, HEAD_DIM))
    got = lax.all_to_all(
        send.reshape(ndp, requests, TILE, HEAD_DIM), DP, split_axis=0, concat_axis=0, tiled=True
    )

    late, weights, grad_rows, _ = lax.optimization_barrier((tokens, w_query, grad_rows, held))
    block = d // nx
    share = [lax.dynamic_slice(late, (SKIP, (mx + by) % nx * block), (length - SKIP, block)) for by in range(nx)]
    share = [split(mc, step(a, "x", by) if by else a, d // ndp) for by, a in enumerate(share)]

    def shifted(array):
        return jnp.concatenate([array[LEAD:], jnp.zeros((LEAD, array.shape[1]), array.dtype)], 0)

    q = shifted(jnp.dot(late, weights, preferred_element_type=F32).astype(BF16))
    g = shifted(grad_rows)
    got, share, q, g = lax.optimization_barrier((got, share, q, g))

    out, dq = attend(q, g, got.reshape(2, heads, tiles, neigh, stretches, TILE, HEAD_DIM))
    dq = jnp.concatenate([jnp.zeros((LEAD - SKIP, width), BF16), dq[:real]], 0)

    mine = other = 0.0
    order = sorted(range(nx), key=lambda by: min(by, nx - by))
    for by in order:
        near = step(dq, "x", by) if by else dq
        if by == 1:
            own = lax.dot_general(dq, fans[0], BOTH_LAST, preferred_element_type=F32).astype(BF16)
            near, own = lax.optimization_barrier((near, own))
        if by == order[-1]:
            near, mine, _ = lax.optimization_barrier((near, mine, other))
        other += lax.dot_general(share[by][1], near, BOTH_FIRST, preferred_element_type=F32)
        mine += lax.dot_general(share[by][0], near, BOTH_FIRST, preferred_element_type=F32)
    mine += step(other, "core", 1)
    groups = jnp.broadcast_to(dq[None], (nmp,) + dq.shape)
    groups = lax.all_to_all(groups, "mp", split_axis=0, concat_axis=0, tiled=True)
    pairs = mine.reshape(nz // 2, 2, -1, width)
    away = lax.dynamic_index_in_dim(pairs, 1 - mz % 2, 1, keepdims=False)
    mine = lax.dynamic_index_in_dim(pairs, mz % 2, 1, keepdims=False)
    up = lax.ppermute(away[..., : width // 2], "z", [(i, i ^ 1) for i in range(nz)])
    down = lax.ppermute(away[..., width // 2 :], "z", [(i, ((i + 1) ^ 1) - 1) for i in range(1, nz - 1)] + [(0, nz - 1), (nz - 1, 0)])
    parts = [own]
    for by in range(1, nmp):
        if by == 2:
            up, parts, groups = lax.optimization_barrier((up, parts, groups))
        near = lax.dynamic_index_in_dim(groups, (my - by) % nmp, 0, keepdims=False)
        parts.append(lax.dot_general(near, fans[by], BOTH_LAST, preferred_element_type=F32).astype(BF16))
    mine += jnp.concatenate([up, down], -1)
    terms = [lax.dynamic_index_in_dim(mine, (mz // 2 + by) % (nz // 2), 0, keepdims=False) for by in range(nz // 2)]
    query_grad = sum(step(a, "z", 2 * by) if by else a for by, a in enumerate(terms))
    part = sum(a.astype(F32) for a in parts).astype(BF16)
    attended = jnp.concatenate([jnp.zeros((LEAD, width), BF16), out[:real]], 0)
    input_grad = jnp.concatenate([jnp.zeros((SKIP, d // nmp), BF16), part], 0)
    return attended[None], input_grad[None], query_grad


def solution(mesh):
    fine = Mesh(mesh.devices.reshape(4, 8, 2, 4), ("x", "z", "core", "mp"))
    return jax.shard_map(
        local,
        mesh=fine,
        in_specs=(
            P(DP, None, None),
            P(None, "mp"),
            P(DP, None, None, "mp"),
            P(DP, None, None),
            P(DP, None, None),
            P(DP, None, "mp"),
        ),
        out_specs=(P(DP, None, "mp"), P(DP, None, "mp"), P(DP, "mp")),
        check_vma=False,
    )
```

```python
import functools

import jax
import jax.numpy as jnp
from jax import lax
from jax.experimental import pallas as pl
from jax.experimental.pallas import tpu as pltpu
from jax.sharding import Mesh
from jax.sharding import PartitionSpec as P

HEAD_DIM = 128
STRETCH = 64
LEAD = STRETCH - 1
TILE = 16
SKIP = LEAD // TILE * TILE
DP = ("x", "z", "core")
VMEM = 32 << 20
BF16, F32 = jnp.bfloat16, jnp.float32
BOTH_LAST = (((1,), (1,)), ((), ()))
BOTH_FIRST = (((0,), (0,)), ((), ()))


def cut_kernel(named_ref, cache_ref, out_ref):
    rows = cache_ref.shape[0]
    _, heads, tiles, _, _, _ = out_ref.shape
    for head in range(heads):
        cols = slice(head * HEAD_DIM, (head + 1) * HEAD_DIM)
        for tile in range(tiles):
            out_ref[0, head, tile, :rows] = cache_ref[:, 0, tile * TILE : (tile + 1) * TILE, cols]
            out_ref[0, head, tile, rows] = named_ref[...]


def cut(named, cache):
    rows, _, nb_len, width = cache.shape
    tiles, heads = nb_len // TILE, width // HEAD_DIM
    return pl.pallas_call(
        cut_kernel,
        grid=(2,),
        in_specs=[
            pl.BlockSpec(named.shape, lambda a: (0, 0)),
            pl.BlockSpec((rows, 1, nb_len, width), lambda a: (0, a, 0, 0)),
        ],
        out_specs=pl.BlockSpec((1, heads, tiles, rows + 1, TILE, HEAD_DIM), lambda a: (a, 0, 0, 0, 0, 0)),
        out_shape=jax.ShapeDtypeStruct((2, heads, tiles, rows + 1, TILE, HEAD_DIM), BF16),
        compiler_params=pltpu.CompilerParams(vmem_limit_bytes=60 << 20),
        cost_estimate=pl.CostEstimate(flops=0, bytes_accessed=4 << 20, transcendentals=0),
        name="cut",
    )(named, cache).reshape(-1, rows + 1, TILE, HEAD_DIM)


def pick_kernel(ids_ref, tiles_ref, out_ref, *, slots):
    base = pl.program_id(0) * slots
    for slot in range(slots):
        out_ref[slot] = tiles_ref[ids_ref[base + slot]]


def pick(ids, tiles):
    count, slots = ids.shape[0], 64
    return pl.pallas_call(
        functools.partial(pick_kernel, slots=slots),
        grid_spec=pltpu.PrefetchScalarGridSpec(
            num_scalar_prefetch=1,
            grid=(count // slots,),
            in_specs=[pl.BlockSpec(tiles.shape, lambda s, ids: (0, 0, 0))],
            out_specs=pl.BlockSpec((slots,) + tiles.shape[1:], lambda s, ids: (s, 0, 0)),
        ),
        out_shape=jax.ShapeDtypeStruct((count,) + tiles.shape[1:], tiles.dtype),
        compiler_params=pltpu.CompilerParams(vmem_limit_bytes=VMEM),
        cost_estimate=pl.CostEstimate(flops=0, bytes_accessed=6 << 20, transcendentals=0),
        name="pick",
    )(ids, tiles)


def attend_kernel(q_ref, g_ref, kv_ref, out_ref, dq_ref, *, heads):
    for i in range(q_ref.shape[0] // STRETCH):
        rows = pl.ds(i * STRETCH, STRETCH)
        kv = kv_ref.at[:, :, :, :, i]
        attend_stretch(q_ref.at[rows], g_ref.at[rows], kv, out_ref.at[rows], dq_ref.at[rows], heads)


def attend_stretch(q_ref, g_ref, kv_ref, out_ref, dq_ref, heads):
    scale = HEAD_DIM ** (-0.5)
    cols = [slice(h * HEAD_DIM, (h + 1) * HEAD_DIM) for h in range(heads)]
    keys = [kv_ref[0, h].reshape(-1, HEAD_DIM) for h in range(heads)]
    values = [kv_ref[1, h].reshape(-1, HEAD_DIM) for h in range(heads)]
    scores = [
        lax.dot_general(q_ref[:, c], k, BOTH_LAST, preferred_element_type=F32)
        for c, k in zip(cols, keys)
    ]
    dprobs = [
        lax.dot_general(g_ref[:, c], v, BOTH_LAST, preferred_element_type=F32)
        for c, v in zip(cols, values)
    ]
    probs, dscores = [], []
    for score, dprob in zip(scores, dprobs):
        score = score * scale
        exps = jnp.exp(score - jnp.max(score, axis=-1, keepdims=True))
        prob = exps * (1.0 / jnp.sum(exps, axis=-1, keepdims=True))
        delta = jnp.sum(dprob * prob, axis=-1, keepdims=True)
        probs.append(prob.astype(BF16))
        dscores.append((prob * (dprob - delta) * scale).astype(BF16))
    for c, k, v, prob, dscore in zip(cols, keys, values, probs, dscores):
        out_ref[:, c] = jnp.dot(prob, v, preferred_element_type=F32).astype(BF16)
        dq_ref[:, c] = jnp.dot(dscore, k, preferred_element_type=F32).astype(BF16)


def attend(q, g, kv):
    rows, width = q.shape
    count, together = rows // STRETCH, 2
    _, heads, tiles, neigh, _, _, _ = kv.shape
    block = pl.BlockSpec((together * STRETCH, width), lambda c: (c, 0))
    return pl.pallas_call(
        functools.partial(attend_kernel, heads=heads),
        grid=(count // together,),
        in_specs=[
            block,
            block,
            pl.BlockSpec(
                (2, heads, tiles, neigh, together, TILE, HEAD_DIM), lambda c: (0, 0, 0, 0, c, 0, 0)
            ),
        ],
        out_specs=[block, block],
        out_shape=[jax.ShapeDtypeStruct(q.shape, BF16)] * 2,
        compiler_params=pltpu.CompilerParams(vmem_limit_bytes=VMEM),
        cost_estimate=pl.CostEstimate(
            flops=10 * rows * width * neigh * tiles * TILE, bytes_accessed=kv.size * 2, transcendentals=0
        ),
        name="attend",
    )(q, g, kv)


def split_kernel(core_ref, share_ref, own_ref, other_ref, *, rows):
    lane = lax.broadcasted_iota(jnp.int32, (share_ref.shape[0], 2 * rows), 1)
    first = core_ref[0] == 0
    for i in range(own_ref.shape[1] // (2 * rows)):
        even = share_ref[:, 4 * i * rows : (4 * i + 2) * rows].astype(F32)
        odd = share_ref[:, (4 * i + 2) * rows : (4 * i + 4) * rows].astype(F32)
        low = jnp.where(lane < rows, even, pltpu.roll(odd, rows, 1)).astype(BF16)
        high = jnp.where(lane < rows, pltpu.roll(even, rows, 1), odd).astype(BF16)
        own_ref[:, 2 * i * rows : 2 * (i + 1) * rows] = jnp.where(first, low, high)
        other_ref[:, 2 * i * rows : 2 * (i + 1) * rows] = jnp.where(first, high, low)


def split(core, share, rows):
    tokens, columns = share.shape
    whole = pl.BlockSpec((tokens, columns // 2), lambda: (0, 0))
    return pl.pallas_call(
        functools.partial(split_kernel, rows=rows),
        in_specs=[pl.BlockSpec(memory_space=pltpu.SMEM), pl.BlockSpec((tokens, columns), lambda: (0, 0))],
        out_specs=[whole] * 2,
        out_shape=[jax.ShapeDtypeStruct((tokens, columns // 2), BF16)] * 2,
        compiler_params=pltpu.CompilerParams(vmem_limit_bytes=16 << 20),
        cost_estimate=pl.CostEstimate(flops=0, bytes_accessed=4 << 20, transcendentals=0),
        name="split",
    )(core.reshape(1), share)


def step(array, axis, by):
    size = lax.axis_size(axis)
    return lax.ppermute(array, axis, [(i, (i + by) % size) for i in range(size)])


def local(inputs, w_query, cache_kv, nb_owner, nb_row, out_grad):
    nx, nz, nc = (lax.axis_size(a) for a in DP)
    ndp, nmp = nx * nz * nc, lax.axis_size("mp")
    mx, mz, mc = (lax.axis_index(a) for a in DP)
    my = lax.axis_index("mp")
    tokens, grad_rows = inputs[0], out_grad[0]
    length, d = tokens.shape
    width = w_query.shape[1]
    heads = width // HEAD_DIM
    db_rows, _, nb_len, _ = cache_kv.shape
    _, stretches, neigh = nb_owner.shape
    requests = stretches * neigh
    tiles = nb_len // TILE
    real = length - LEAD

    lanes = (0, HEAD_DIM - stretches)
    named = jnp.pad(nb_owner[0].T, ((0, TILE - neigh), lanes)) + jnp.pad(nb_row[0].T, ((neigh, TILE - 2 * neigh), lanes))
    message = cut(named.astype(BF16), cache_kv)
    held = lax.all_to_all(message, DP, split_axis=0, concat_axis=0, tiled=True)

    block = d // nmp
    fans = [lax.dynamic_slice(w_query, ((my + by) % nmp * block, 0), (block, width)) for by in range(nmp)]
    fans = [step(a, "mp", by) if by else a for by, a in enumerate(fans)]
    held, fans = lax.optimization_barrier((held, fans))

    named = held[:, db_rows, : 2 * neigh, :stretches].astype(jnp.int32)
    ids = named[:, :neigh] * (db_rows + 1) + named[:, neigh:]
    send = pick(ids.reshape(-1), held.reshape(-1, TILE, HEAD_DIM))
    got = lax.all_to_all(
        send.reshape(ndp, requests, TILE, HEAD_DIM), DP, split_axis=0, concat_axis=0, tiled=True
    )

    late, weights, grad_rows, _ = lax.optimization_barrier((tokens, w_query, grad_rows, held))
    block = d // nx
    share = [lax.dynamic_slice(late, (SKIP, (mx + by) % nx * block), (length - SKIP, block)) for by in range(nx)]
    share = [split(mc, step(a, "x", by) if by else a, d // ndp) for by, a in enumerate(share)]

    def shifted(array):
        return jnp.concatenate([array[LEAD:], jnp.zeros((LEAD, array.shape[1]), array.dtype)], 0)

    q = shifted(jnp.dot(late, weights, preferred_element_type=F32).astype(BF16))
    g = shifted(grad_rows)
    got, share, q, g = lax.optimization_barrier((got, share, q, g))

    out, dq = attend(q, g, got.reshape(2, heads, tiles, neigh, stretches, TILE, HEAD_DIM))
    dq = jnp.concatenate([jnp.zeros((LEAD - SKIP, width), BF16), dq[:real]], 0)

    groups = [step(dq, "mp", by) if by else dq for by in range(nmp)]
    mine = other = 0.0
    order = sorted(range(nx), key=lambda by: min(by, nx - by))
    for by in order:
        near = step(dq, "x", by) if by else dq
        if by == 1:
            own = lax.dot_general(dq, fans[0], BOTH_LAST, preferred_element_type=F32).astype(BF16)
            near, own = lax.optimization_barrier((near, own))
        if by == order[-1]:
            near, mine, groups[1], _ = lax.optimization_barrier((near, mine, groups[1], other))
        other += lax.dot_general(share[by][1], near, BOTH_FIRST, preferred_element_type=F32)
        mine += lax.dot_general(share[by][0], near, BOTH_FIRST, preferred_element_type=F32)
    mine += step(other, "core", 1)
    pairs = mine.reshape(nz // 2, 2, -1, width)
    away = lax.dynamic_index_in_dim(pairs, 1 - mz % 2, 1, keepdims=False)
    mine = lax.dynamic_index_in_dim(pairs, mz % 2, 1, keepdims=False)
    up = lax.ppermute(away[..., : width // 2], "z", [(i, i ^ 1) for i in range(nz)])
    down = lax.ppermute(away[..., width // 2 :], "z", [(i, ((i + 1) ^ 1) - 1) for i in range(1, nz - 1)] + [(0, nz - 1), (nz - 1, 0)])
    parts = [own, lax.dot_general(groups[1], fans[1], BOTH_LAST, preferred_element_type=F32).astype(BF16)]
    up, parts = lax.optimization_barrier((up, parts))
    late, _ = lax.optimization_barrier((groups[2:], up))
    for by, near in enumerate(late, 2):
        parts.append(lax.dot_general(near, fans[by], BOTH_LAST, preferred_element_type=F32).astype(BF16))
    mine += jnp.concatenate([up, down], -1)
    terms = [lax.dynamic_index_in_dim(mine, (mz // 2 + by) % (nz // 2), 0, keepdims=False) for by in range(nz // 2)]
    query_grad = sum(step(a, "z", 2 * by) if by else a for by, a in enumerate(terms))
    part = sum(a.astype(F32) for a in parts).astype(BF16)
    attended = jnp.concatenate([jnp.zeros((LEAD, width), BF16), out[:real]], 0)
    input_grad = jnp.concatenate([jnp.zeros((SKIP, d // nmp), BF16), part], 0)
    return attended[None], input_grad[None], query_grad


def solution(mesh):
    fine = Mesh(mesh.devices.reshape(4, 8, 2, 4), ("x", "z", "core", "mp"))
    return jax.shard_map(
        local,
        mesh=fine,
        in_specs=(
            P(DP, None, None),
            P(None, "mp"),
            P(DP, None, None, "mp"),
            P(DP, None, None),
            P(DP, None, None),
            P(DP, None, "mp"),
        ),
        out_specs=(P(DP, None, "mp"), P(DP, None, "mp"), P(DP, "mp")),
        check_vma=False,
    )
```

```python
import functools

import jax
import jax.numpy as jnp
from jax import lax
from jax.experimental import pallas as pl
from jax.experimental.pallas import tpu as pltpu
from jax.sharding import Mesh
from jax.sharding import PartitionSpec as P

HEAD_DIM = 128
STRETCH = 64
LEAD = STRETCH - 1
TILE = 16
SKIP = LEAD // TILE * TILE
DP = ("x", "z", "core")
VMEM = 32 << 20
BF16, F32 = jnp.bfloat16, jnp.float32
BOTH_LAST = (((1,), (1,)), ((), ()))
BOTH_FIRST = (((0,), (0,)), ((), ()))


def cut_kernel(named_ref, cache_ref, out_ref):
    rows = cache_ref.shape[0]
    _, heads, tiles, _, _, _ = out_ref.shape
    for head in range(heads):
        cols = slice(head * HEAD_DIM, (head + 1) * HEAD_DIM)
        for tile in range(tiles):
            out_ref[0, head, tile, :rows] = cache_ref[:, 0, tile * TILE : (tile + 1) * TILE, cols]
            out_ref[0, head, tile, rows] = named_ref[...]


def cut(named, cache):
    rows, _, nb_len, width = cache.shape
    tiles, heads = nb_len // TILE, width // HEAD_DIM
    return pl.pallas_call(
        cut_kernel,
        grid=(2,),
        in_specs=[
            pl.BlockSpec(named.shape, lambda a: (0, 0)),
            pl.BlockSpec((rows, 1, nb_len, width), lambda a: (0, a, 0, 0)),
        ],
        out_specs=pl.BlockSpec((1, heads, tiles, rows + 1, TILE, HEAD_DIM), lambda a: (a, 0, 0, 0, 0, 0)),
        out_shape=jax.ShapeDtypeStruct((2, heads, tiles, rows + 1, TILE, HEAD_DIM), BF16),
        compiler_params=pltpu.CompilerParams(vmem_limit_bytes=60 << 20),
        cost_estimate=pl.CostEstimate(flops=0, bytes_accessed=4 << 20, transcendentals=0),
        name="cut",
    )(named, cache).reshape(-1, rows + 1, TILE, HEAD_DIM)


def pick_kernel(ids_ref, tiles_ref, out_ref, *, slots):
    base = pl.program_id(0) * slots
    for slot in range(slots):
        out_ref[slot] = tiles_ref[ids_ref[base + slot]]


def pick(ids, tiles):
    count, slots = ids.shape[0], 64
    return pl.pallas_call(
        functools.partial(pick_kernel, slots=slots),
        grid_spec=pltpu.PrefetchScalarGridSpec(
            num_scalar_prefetch=1,
            grid=(count // slots,),
            in_specs=[pl.BlockSpec(tiles.shape, lambda s, ids: (0, 0, 0))],
            out_specs=pl.BlockSpec((slots,) + tiles.shape[1:], lambda s, ids: (s, 0, 0)),
        ),
        out_shape=jax.ShapeDtypeStruct((count,) + tiles.shape[1:], tiles.dtype),
        compiler_params=pltpu.CompilerParams(vmem_limit_bytes=VMEM),
        cost_estimate=pl.CostEstimate(flops=0, bytes_accessed=6 << 20, transcendentals=0),
        name="pick",
    )(ids, tiles)


def attend_kernel(q_ref, g_ref, kv_ref, out_ref, dq_ref, *, heads):
    for i in range(q_ref.shape[0] // STRETCH):
        rows = pl.ds(i * STRETCH, STRETCH)
        kv = kv_ref.at[:, :, :, :, i]
        attend_stretch(q_ref.at[rows], g_ref.at[rows], kv, out_ref.at[rows], dq_ref.at[rows], heads)


def attend_stretch(q_ref, g_ref, kv_ref, out_ref, dq_ref, heads):
    scale = HEAD_DIM ** (-0.5)
    cols = [slice(h * HEAD_DIM, (h + 1) * HEAD_DIM) for h in range(heads)]
    keys = [kv_ref[0, h].reshape(-1, HEAD_DIM) for h in range(heads)]
    values = [kv_ref[1, h].reshape(-1, HEAD_DIM) for h in range(heads)]
    scores = [
        lax.dot_general(q_ref[:, c], k, BOTH_LAST, preferred_element_type=F32)
        for c, k in zip(cols, keys)
    ]
    dprobs = [
        lax.dot_general(g_ref[:, c], v, BOTH_LAST, preferred_element_type=F32)
        for c, v in zip(cols, values)
    ]
    probs, dscores = [], []
    for score, dprob in zip(scores, dprobs):
        score = score * scale
        exps = jnp.exp(score - jnp.max(score, axis=-1, keepdims=True))
        prob = exps * (1.0 / jnp.sum(exps, axis=-1, keepdims=True))
        delta = jnp.sum(dprob * prob, axis=-1, keepdims=True)
        probs.append(prob.astype(BF16))
        dscores.append((prob * (dprob - delta) * scale).astype(BF16))
    for c, k, v, prob, dscore in zip(cols, keys, values, probs, dscores):
        out_ref[:, c] = jnp.dot(prob, v, preferred_element_type=F32).astype(BF16)
        dq_ref[:, c] = jnp.dot(dscore, k, preferred_element_type=F32).astype(BF16)


def attend(q, g, kv):
    rows, width = q.shape
    count, together = rows // STRETCH, 2
    _, heads, tiles, neigh, _, _, _ = kv.shape
    block = pl.BlockSpec((together * STRETCH, width), lambda c: (c, 0))
    return pl.pallas_call(
        functools.partial(attend_kernel, heads=heads),
        grid=(count // together,),
        in_specs=[
            block,
            block,
            pl.BlockSpec(
                (2, heads, tiles, neigh, together, TILE, HEAD_DIM), lambda c: (0, 0, 0, 0, c, 0, 0)
            ),
        ],
        out_specs=[block, block],
        out_shape=[jax.ShapeDtypeStruct(q.shape, BF16)] * 2,
        compiler_params=pltpu.CompilerParams(vmem_limit_bytes=VMEM),
        cost_estimate=pl.CostEstimate(
            flops=10 * rows * width * neigh * tiles * TILE, bytes_accessed=kv.size * 2, transcendentals=0
        ),
        name="attend",
    )(q, g, kv)


def split_kernel(core_ref, share_ref, own_ref, other_ref, *, rows):
    lane = lax.broadcasted_iota(jnp.int32, (share_ref.shape[0], 2 * rows), 1)
    first = core_ref[0] == 0
    for i in range(own_ref.shape[1] // (2 * rows)):
        even = share_ref[:, 4 * i * rows : (4 * i + 2) * rows].astype(F32)
        odd = share_ref[:, (4 * i + 2) * rows : (4 * i + 4) * rows].astype(F32)
        low = jnp.where(lane < rows, even, pltpu.roll(odd, rows, 1)).astype(BF16)
        high = jnp.where(lane < rows, pltpu.roll(even, rows, 1), odd).astype(BF16)
        own_ref[:, 2 * i * rows : 2 * (i + 1) * rows] = jnp.where(first, low, high)
        other_ref[:, 2 * i * rows : 2 * (i + 1) * rows] = jnp.where(first, high, low)


def split(core, share, rows):
    tokens, columns = share.shape
    whole = pl.BlockSpec((tokens, columns // 2), lambda: (0, 0))
    return pl.pallas_call(
        functools.partial(split_kernel, rows=rows),
        in_specs=[pl.BlockSpec(memory_space=pltpu.SMEM), pl.BlockSpec((tokens, columns), lambda: (0, 0))],
        out_specs=[whole] * 2,
        out_shape=[jax.ShapeDtypeStruct((tokens, columns // 2), BF16)] * 2,
        compiler_params=pltpu.CompilerParams(vmem_limit_bytes=16 << 20),
        cost_estimate=pl.CostEstimate(flops=0, bytes_accessed=4 << 20, transcendentals=0),
        name="split",
    )(core.reshape(1), share)


def step(array, axis, by):
    size = lax.axis_size(axis)
    return lax.ppermute(array, axis, [(i, (i + by) % size) for i in range(size)])


def local(inputs, w_query, cache_kv, nb_owner, nb_row, out_grad):
    nx, nz, nc = (lax.axis_size(a) for a in DP)
    ndp, nmp = nx * nz * nc, lax.axis_size("mp")
    mx, mz, mc = (lax.axis_index(a) for a in DP)
    my = lax.axis_index("mp")
    tokens, grad_rows = inputs[0], out_grad[0]
    length, d = tokens.shape
    width = w_query.shape[1]
    heads = width // HEAD_DIM
    db_rows, _, nb_len, _ = cache_kv.shape
    _, stretches, neigh = nb_owner.shape
    requests = stretches * neigh
    tiles = nb_len // TILE
    real = length - LEAD

    lanes = (0, HEAD_DIM - stretches)
    named = jnp.pad(nb_owner[0].T, ((0, TILE - neigh), lanes)) + jnp.pad(nb_row[0].T, ((neigh, TILE - 2 * neigh), lanes))
    message = cut(named.astype(BF16), cache_kv)
    held = lax.all_to_all(message, DP, split_axis=0, concat_axis=0, tiled=True)

    block = d // nmp
    fans = [lax.dynamic_slice(w_query, ((my + by) % nmp * block, 0), (block, width)) for by in range(nmp)]
    fans = [step(a, "mp", by) if by else a for by, a in enumerate(fans)]
    held, fans = lax.optimization_barrier((held, fans))

    named = held[:, db_rows, : 2 * neigh, :stretches].astype(jnp.int32)
    ids = named[:, :neigh] * (db_rows + 1) + named[:, neigh:]
    send = pick(ids.reshape(-1), held.reshape(-1, TILE, HEAD_DIM))
    got = lax.all_to_all(
        send.reshape(ndp, requests, TILE, HEAD_DIM), DP, split_axis=0, concat_axis=0, tiled=True
    )

    late, weights, grad_rows, _ = lax.optimization_barrier((tokens, w_query, grad_rows, held))
    block = d // nx
    share = [lax.dynamic_slice(late, (SKIP, (mx + by) % nx * block), (length - SKIP, block)) for by in range(nx)]
    share = [split(mc, step(a, "x", by) if by else a, d // ndp) for by, a in enumerate(share)]

    def shifted(array):
        return jnp.concatenate([array[LEAD:], jnp.zeros((LEAD, array.shape[1]), array.dtype)], 0)

    q = shifted(jnp.dot(late, weights, preferred_element_type=F32).astype(BF16))
    g = shifted(grad_rows)
    got, share, q, g = lax.optimization_barrier((got, share, q, g))

    out, dq = attend(q, g, got.reshape(2, heads, tiles, neigh, stretches, TILE, HEAD_DIM))
    dq = jnp.concatenate([jnp.zeros((LEAD - SKIP, width), BF16), dq[:real]], 0)

    groups = [step(dq, "mp", by) if by else dq for by in range(nmp)]
    mine = other = 0.0
    order = sorted(range(nx), key=lambda by: min(by, nx - by))
    for by in order:
        near = step(dq, "x", by) if by else dq
        if by == 1:
            own = lax.dot_general(dq, fans[0], BOTH_LAST, preferred_element_type=F32).astype(BF16)
            near, own = lax.optimization_barrier((near, own))
        if by == order[-1]:
            near, mine, groups[1], _ = lax.optimization_barrier((near, mine, groups[1], other))
        other += lax.dot_general(share[by][1], near, BOTH_FIRST, preferred_element_type=F32)
        mine += lax.dot_general(share[by][0], near, BOTH_FIRST, preferred_element_type=F32)
    mine += step(other, "core", 1)
    pairs = mine.reshape(nz // 2, 2, -1, width)
    away = lax.dynamic_index_in_dim(pairs, 1 - mz % 2, 1, keepdims=False)
    mine = lax.dynamic_index_in_dim(pairs, mz % 2, 1, keepdims=False)
    up = lax.ppermute(away[..., : width // 2], "z", [(i, i ^ 1) for i in range(nz)])
    down = lax.ppermute(away[..., width // 2 :], "z", [(i, ((i + 1) ^ 1) - 1) for i in range(1, nz - 1)] + [(0, nz - 1), (nz - 1, 0)])
    parts = [own, lax.dot_general(groups[1], fans[1], BOTH_LAST, preferred_element_type=F32).astype(BF16)]
    up, parts = lax.optimization_barrier((up, parts))
    mine += jnp.concatenate([up, down], -1)
    terms = [lax.dynamic_index_in_dim(mine, (mz // 2 + by) % (nz // 2), 0, keepdims=False) for by in range(nz // 2)]
    terms = [step(a, "z", 2 * by) if by else a for by, a in enumerate(terms)]
    late, _ = lax.optimization_barrier((groups[2:], terms[1]))
    for by, near in enumerate(late, 2):
        parts.append(lax.dot_general(near, fans[by], BOTH_LAST, preferred_element_type=F32).astype(BF16))
    query_grad = sum(terms)
    part = sum(a.astype(F32) for a in parts).astype(BF16)
    attended = jnp.concatenate([jnp.zeros((LEAD, width), BF16), out[:real]], 0)
    input_grad = jnp.concatenate([jnp.zeros((SKIP, d // nmp), BF16), part], 0)
    return attended[None], input_grad[None], query_grad


def solution(mesh):
    fine = Mesh(mesh.devices.reshape(4, 8, 2, 4), ("x", "z", "core", "mp"))
    return jax.shard_map(
        local,
        mesh=fine,
        in_specs=(
            P(DP, None, None),
            P(None, "mp"),
            P(DP, None, None, "mp"),
            P(DP, None, None),
            P(DP, None, None),
            P(DP, None, "mp"),
        ),
        out_specs=(P(DP, None, "mp"), P(DP, None, "mp"), P(DP, "mp")),
        check_vma=False,
    )
```

```python
import functools

import jax
import jax.numpy as jnp
from jax import lax
from jax.experimental import pallas as pl
from jax.experimental.pallas import tpu as pltpu
from jax.sharding import Mesh
from jax.sharding import PartitionSpec as P

HEAD_DIM = 128
STRETCH = 64
LEAD = STRETCH - 1
TILE = 16
SKIP = LEAD // TILE * TILE
DP = ("x", "z", "core")
VMEM = 32 << 20
BF16, F32 = jnp.bfloat16, jnp.float32
BOTH_LAST = (((1,), (1,)), ((), ()))
BOTH_FIRST = (((0,), (0,)), ((), ()))


def cut_kernel(named_ref, cache_ref, out_ref):
    rows = cache_ref.shape[0]
    _, heads, tiles, _, _, _ = out_ref.shape
    for head in range(heads):
        cols = slice(head * HEAD_DIM, (head + 1) * HEAD_DIM)
        for tile in range(tiles):
            out_ref[0, head, tile, :rows] = cache_ref[:, 0, tile * TILE : (tile + 1) * TILE, cols]
            out_ref[0, head, tile, rows] = named_ref[...]


def cut(named, cache):
    rows, _, nb_len, width = cache.shape
    tiles, heads = nb_len // TILE, width // HEAD_DIM
    return pl.pallas_call(
        cut_kernel,
        grid=(2,),
        in_specs=[
            pl.BlockSpec(named.shape, lambda a: (0, 0)),
            pl.BlockSpec((rows, 1, nb_len, width), lambda a: (0, a, 0, 0)),
        ],
        out_specs=pl.BlockSpec((1, heads, tiles, rows + 1, TILE, HEAD_DIM), lambda a: (a, 0, 0, 0, 0, 0)),
        out_shape=jax.ShapeDtypeStruct((2, heads, tiles, rows + 1, TILE, HEAD_DIM), BF16),
        compiler_params=pltpu.CompilerParams(vmem_limit_bytes=60 << 20),
        cost_estimate=pl.CostEstimate(flops=0, bytes_accessed=4 << 20, transcendentals=0),
        name="cut",
    )(named, cache).reshape(-1, rows + 1, TILE, HEAD_DIM)


def pick_kernel(ids_ref, tiles_ref, out_ref, *, slots):
    base = pl.program_id(0) * slots
    for slot in range(slots):
        out_ref[slot] = tiles_ref[ids_ref[base + slot]]


def pick(ids, tiles):
    count, slots = ids.shape[0], 64
    return pl.pallas_call(
        functools.partial(pick_kernel, slots=slots),
        grid_spec=pltpu.PrefetchScalarGridSpec(
            num_scalar_prefetch=1,
            grid=(count // slots,),
            in_specs=[pl.BlockSpec(tiles.shape, lambda s, ids: (0, 0, 0))],
            out_specs=pl.BlockSpec((slots,) + tiles.shape[1:], lambda s, ids: (s, 0, 0)),
        ),
        out_shape=jax.ShapeDtypeStruct((count,) + tiles.shape[1:], tiles.dtype),
        compiler_params=pltpu.CompilerParams(vmem_limit_bytes=VMEM),
        cost_estimate=pl.CostEstimate(flops=0, bytes_accessed=6 << 20, transcendentals=0),
        name="pick",
    )(ids, tiles)


def attend_kernel(q_ref, g_ref, kv_ref, out_ref, dq_ref, *, heads):
    for i in range(q_ref.shape[0] // STRETCH):
        rows = pl.ds(i * STRETCH, STRETCH)
        kv = kv_ref.at[:, :, :, :, i]
        attend_stretch(q_ref.at[rows], g_ref.at[rows], kv, out_ref.at[rows], dq_ref.at[rows], heads)


def attend_stretch(q_ref, g_ref, kv_ref, out_ref, dq_ref, heads):
    scale = HEAD_DIM ** (-0.5)
    cols = [slice(h * HEAD_DIM, (h + 1) * HEAD_DIM) for h in range(heads)]
    keys = [kv_ref[0, h].reshape(-1, HEAD_DIM) for h in range(heads)]
    values = [kv_ref[1, h].reshape(-1, HEAD_DIM) for h in range(heads)]
    scores = [
        lax.dot_general(q_ref[:, c], k, BOTH_LAST, preferred_element_type=F32)
        for c, k in zip(cols, keys)
    ]
    dprobs = [
        lax.dot_general(g_ref[:, c], v, BOTH_LAST, preferred_element_type=F32)
        for c, v in zip(cols, values)
    ]
    probs, dscores = [], []
    for score, dprob in zip(scores, dprobs):
        score = score * scale
        exps = jnp.exp(score - jnp.max(score, axis=-1, keepdims=True))
        prob = exps * (1.0 / jnp.sum(exps, axis=-1, keepdims=True))
        delta = jnp.sum(dprob * prob, axis=-1, keepdims=True)
        probs.append(prob.astype(BF16))
        dscores.append((prob * (dprob - delta) * scale).astype(BF16))
    for c, k, v, prob, dscore in zip(cols, keys, values, probs, dscores):
        out_ref[:, c] = jnp.dot(prob, v, preferred_element_type=F32).astype(BF16)
        dq_ref[:, c] = jnp.dot(dscore, k, preferred_element_type=F32).astype(BF16)


def attend(q, g, kv):
    rows, width = q.shape
    count, together = rows // STRETCH, 2
    _, heads, tiles, neigh, _, _, _ = kv.shape
    block = pl.BlockSpec((together * STRETCH, width), lambda c: (c, 0))
    return pl.pallas_call(
        functools.partial(attend_kernel, heads=heads),
        grid=(count // together,),
        in_specs=[
            block,
            block,
            pl.BlockSpec(
                (2, heads, tiles, neigh, together, TILE, HEAD_DIM), lambda c: (0, 0, 0, 0, c, 0, 0)
            ),
        ],
        out_specs=[block, block],
        out_shape=[jax.ShapeDtypeStruct(q.shape, BF16)] * 2,
        compiler_params=pltpu.CompilerParams(vmem_limit_bytes=VMEM),
        cost_estimate=pl.CostEstimate(
            flops=10 * rows * width * neigh * tiles * TILE, bytes_accessed=kv.size * 2, transcendentals=0
        ),
        name="attend",
    )(q, g, kv)


def split_kernel(core_ref, share_ref, own_ref, other_ref, *, rows):
    lane = lax.broadcasted_iota(jnp.int32, (share_ref.shape[0], 2 * rows), 1)
    first = core_ref[0] == 0
    for i in range(own_ref.shape[1] // (2 * rows)):
        even = share_ref[:, 4 * i * rows : (4 * i + 2) * rows].astype(F32)
        odd = share_ref[:, (4 * i + 2) * rows : (4 * i + 4) * rows].astype(F32)
        low = jnp.where(lane < rows, even, pltpu.roll(odd, rows, 1)).astype(BF16)
        high = jnp.where(lane < rows, pltpu.roll(even, rows, 1), odd).astype(BF16)
        own_ref[:, 2 * i * rows : 2 * (i + 1) * rows] = jnp.where(first, low, high)
        other_ref[:, 2 * i * rows : 2 * (i + 1) * rows] = jnp.where(first, high, low)


def split(core, share, rows):
    tokens, columns = share.shape
    whole = pl.BlockSpec((tokens, columns // 2), lambda: (0, 0))
    return pl.pallas_call(
        functools.partial(split_kernel, rows=rows),
        in_specs=[pl.BlockSpec(memory_space=pltpu.SMEM), pl.BlockSpec((tokens, columns), lambda: (0, 0))],
        out_specs=[whole] * 2,
        out_shape=[jax.ShapeDtypeStruct((tokens, columns // 2), BF16)] * 2,
        compiler_params=pltpu.CompilerParams(vmem_limit_bytes=16 << 20),
        cost_estimate=pl.CostEstimate(flops=0, bytes_accessed=4 << 20, transcendentals=0),
        name="split",
    )(core.reshape(1), share)


def step(array, axis, by):
    size = lax.axis_size(axis)
    return lax.ppermute(array, axis, [(i, (i + by) % size) for i in range(size)])


def local(inputs, w_query, cache_kv, nb_owner, nb_row, out_grad):
    nx, nz, nc = (lax.axis_size(a) for a in DP)
    ndp, nmp = nx * nz * nc, lax.axis_size("mp")
    mx, mz, mc = (lax.axis_index(a) for a in DP)
    my = lax.axis_index("mp")
    tokens, grad_rows = inputs[0], out_grad[0]
    length, d = tokens.shape
    width = w_query.shape[1]
    heads = width // HEAD_DIM
    db_rows, _, nb_len, _ = cache_kv.shape
    _, stretches, neigh = nb_owner.shape
    requests = stretches * neigh
    tiles = nb_len // TILE
    real = length - LEAD

    lanes = (0, HEAD_DIM - stretches)
    named = jnp.pad(nb_owner[0].T, ((0, TILE - neigh), lanes)) + jnp.pad(nb_row[0].T, ((neigh, TILE - 2 * neigh), lanes))
    message = cut(named.astype(BF16), cache_kv)
    held = lax.all_to_all(message, DP, split_axis=0, concat_axis=0, tiled=True)

    block = d // nmp
    fans = [lax.dynamic_slice(w_query, ((my + by) % nmp * block, 0), (block, width)) for by in range(nmp)]
    fans = [step(a, "mp", by) if by else a for by, a in enumerate(fans)]
    held, fans = lax.optimization_barrier((held, fans))

    named = held[:, db_rows, : 2 * neigh, :stretches].astype(jnp.int32)
    ids = named[:, :neigh] * (db_rows + 1) + named[:, neigh:]
    send = pick(ids.reshape(-1), held.reshape(-1, TILE, HEAD_DIM))
    got = lax.all_to_all(
        send.reshape(ndp, requests, TILE, HEAD_DIM), DP, split_axis=0, concat_axis=0, tiled=True
    )

    late, weights, grad_rows, _ = lax.optimization_barrier((tokens, w_query, grad_rows, held))
    block = d // nx
    share = [lax.dynamic_slice(late, (SKIP, (mx + by) % nx * block), (length - SKIP, block)) for by in range(nx)]
    share = [split(mc, step(a, "x", by) if by else a, d // ndp) for by, a in enumerate(share)]

    def shifted(array):
        return jnp.concatenate([array[LEAD:], jnp.zeros((LEAD, array.shape[1]), array.dtype)], 0)

    q = shifted(jnp.dot(late, weights, preferred_element_type=F32).astype(BF16))
    g = shifted(grad_rows)
    got, share, q, g = lax.optimization_barrier((got, share, q, g))

    out, dq = attend(q, g, got.reshape(2, heads, tiles, neigh, stretches, TILE, HEAD_DIM))
    dq = jnp.concatenate([jnp.zeros((LEAD - SKIP, width), BF16), dq[:real]], 0)

    groups = [step(dq, "mp", by) if by else dq for by in range(nmp)]
    mine = other = 0.0
    order = sorted(range(nx), key=lambda by: min(by, nx - by))
    for by in order:
        near = step(dq, "x", by) if by else dq
        if by == 1:
            own = lax.dot_general(dq, fans[0], BOTH_LAST, preferred_element_type=F32).astype(BF16)
            near, own = lax.optimization_barrier((near, own))
        if by == order[-1]:
            near, mine, groups[1], _ = lax.optimization_barrier((near, mine, groups[1], other))
        other += lax.dot_general(share[by][1], near, BOTH_FIRST, preferred_element_type=F32)
        mine += lax.dot_general(share[by][0], near, BOTH_FIRST, preferred_element_type=F32)
    mine += step(other, "core", 1)
    pairs = mine.reshape(nz // 2, 2, -1, width)
    away = lax.dynamic_index_in_dim(pairs, 1 - mz % 2, 1, keepdims=False)
    mine = lax.dynamic_index_in_dim(pairs, mz % 2, 1, keepdims=False)
    up = lax.ppermute(away[..., : width // 2], "z", [(i, i ^ 1) for i in range(nz)])
    down = lax.ppermute(away[..., width // 2 :], "z", [(i, ((i + 1) ^ 1) - 1) for i in range(1, nz - 1)] + [(0, nz - 1), (nz - 1, 0)])
    parts = [own, lax.dot_general(groups[1], fans[1], BOTH_LAST, preferred_element_type=F32).astype(BF16)]
    up, parts = lax.optimization_barrier((up, parts))
    mine += jnp.concatenate([up, down], -1)
    terms = [lax.dynamic_index_in_dim(mine, (mz // 2 + by) % (nz // 2), 0, keepdims=False) for by in range(nz // 2)]
    terms = [step(a, "z", 2 * by) if by else a for by, a in enumerate(terms)]
    late, _ = lax.optimization_barrier((groups[2:], mine))
    for by, near in enumerate(late, 2):
        parts.append(lax.dot_general(near, fans[by], BOTH_LAST, preferred_element_type=F32).astype(BF16))
    query_grad = sum(terms)
    part = sum(a.astype(F32) for a in parts).astype(BF16)
    attended = jnp.concatenate([jnp.zeros((LEAD, width), BF16), out[:real]], 0)
    input_grad = jnp.concatenate([jnp.zeros((SKIP, d // nmp), BF16), part], 0)
    return attended[None], input_grad[None], query_grad


def solution(mesh):
    fine = Mesh(mesh.devices.reshape(4, 8, 2, 4), ("x", "z", "core", "mp"))
    return jax.shard_map(
        local,
        mesh=fine,
        in_specs=(
            P(DP, None, None),
            P(None, "mp"),
            P(DP, None, None, "mp"),
            P(DP, None, None),
            P(DP, None, None),
            P(DP, None, "mp"),
        ),
        out_specs=(P(DP, None, "mp"), P(DP, None, "mp"), P(DP, "mp")),
        check_vma=False,
    )
```

```python
import functools

import jax
import jax.numpy as jnp
from jax import lax
from jax.experimental import pallas as pl
from jax.experimental.pallas import tpu as pltpu
from jax.sharding import Mesh
from jax.sharding import PartitionSpec as P

HEAD_DIM = 128
STRETCH = 64
LEAD = STRETCH - 1
TILE = 16
SKIP = LEAD // TILE * TILE
DP = ("x", "z", "core")
VMEM = 32 << 20
BF16, F32 = jnp.bfloat16, jnp.float32
BOTH_LAST = (((1,), (1,)), ((), ()))
BOTH_FIRST = (((0,), (0,)), ((), ()))


def cut_kernel(named_ref, cache_ref, out_ref):
    rows = cache_ref.shape[0]
    _, heads, tiles, _, _, _ = out_ref.shape
    for head in range(heads):
        cols = slice(head * HEAD_DIM, (head + 1) * HEAD_DIM)
        for tile in range(tiles):
            out_ref[0, head, tile, :rows] = cache_ref[:, 0, tile * TILE : (tile + 1) * TILE, cols]
            out_ref[0, head, tile, rows] = named_ref[...]


def cut(named, cache):
    rows, _, nb_len, width = cache.shape
    tiles, heads = nb_len // TILE, width // HEAD_DIM
    return pl.pallas_call(
        cut_kernel,
        grid=(2,),
        in_specs=[
            pl.BlockSpec(named.shape, lambda a: (0, 0)),
            pl.BlockSpec((rows, 1, nb_len, width), lambda a: (0, a, 0, 0)),
        ],
        out_specs=pl.BlockSpec((1, heads, tiles, rows + 1, TILE, HEAD_DIM), lambda a: (a, 0, 0, 0, 0, 0)),
        out_shape=jax.ShapeDtypeStruct((2, heads, tiles, rows + 1, TILE, HEAD_DIM), BF16),
        compiler_params=pltpu.CompilerParams(vmem_limit_bytes=60 << 20),
        cost_estimate=pl.CostEstimate(flops=0, bytes_accessed=4 << 20, transcendentals=0),
        name="cut",
    )(named, cache).reshape(-1, rows + 1, TILE, HEAD_DIM)


def pick_kernel(ids_ref, tiles_ref, out_ref, *, slots):
    base = pl.program_id(0) * slots
    for slot in range(slots):
        out_ref[slot] = tiles_ref[ids_ref[base + slot]]


def pick(ids, tiles):
    count, slots = ids.shape[0], 64
    return pl.pallas_call(
        functools.partial(pick_kernel, slots=slots),
        grid_spec=pltpu.PrefetchScalarGridSpec(
            num_scalar_prefetch=1,
            grid=(count // slots,),
            in_specs=[pl.BlockSpec(tiles.shape, lambda s, ids: (0, 0, 0))],
            out_specs=pl.BlockSpec((slots,) + tiles.shape[1:], lambda s, ids: (s, 0, 0)),
        ),
        out_shape=jax.ShapeDtypeStruct((count,) + tiles.shape[1:], tiles.dtype),
        compiler_params=pltpu.CompilerParams(vmem_limit_bytes=VMEM),
        cost_estimate=pl.CostEstimate(flops=0, bytes_accessed=6 << 20, transcendentals=0),
        name="pick",
    )(ids, tiles)


def attend_kernel(q_ref, g_ref, kv_ref, out_ref, dq_ref, *, heads):
    for i in range(q_ref.shape[0] // STRETCH):
        rows = pl.ds(i * STRETCH, STRETCH)
        kv = kv_ref.at[:, :, :, :, i]
        attend_stretch(q_ref.at[rows], g_ref.at[rows], kv, out_ref.at[rows], dq_ref.at[rows], heads)


def attend_stretch(q_ref, g_ref, kv_ref, out_ref, dq_ref, heads):
    scale = HEAD_DIM ** (-0.5)
    cols = [slice(h * HEAD_DIM, (h + 1) * HEAD_DIM) for h in range(heads)]
    keys = [kv_ref[0, h].reshape(-1, HEAD_DIM) for h in range(heads)]
    values = [kv_ref[1, h].reshape(-1, HEAD_DIM) for h in range(heads)]
    scores = [
        lax.dot_general(q_ref[:, c], k, BOTH_LAST, preferred_element_type=F32)
        for c, k in zip(cols, keys)
    ]
    dprobs = [
        lax.dot_general(g_ref[:, c], v, BOTH_LAST, preferred_element_type=F32)
        for c, v in zip(cols, values)
    ]
    probs, dscores = [], []
    for score, dprob in zip(scores, dprobs):
        score = score * scale
        exps = jnp.exp(score - jnp.max(score, axis=-1, keepdims=True))
        prob = exps * (1.0 / jnp.sum(exps, axis=-1, keepdims=True))
        delta = jnp.sum(dprob * prob, axis=-1, keepdims=True)
        probs.append(prob.astype(BF16))
        dscores.append((prob * (dprob - delta) * scale).astype(BF16))
    for c, k, v, prob, dscore in zip(cols, keys, values, probs, dscores):
        out_ref[:, c] = jnp.dot(prob, v, preferred_element_type=F32).astype(BF16)
        dq_ref[:, c] = jnp.dot(dscore, k, preferred_element_type=F32).astype(BF16)


def attend(q, g, kv):
    rows, width = q.shape
    count, together = rows // STRETCH, 2
    _, heads, tiles, neigh, _, _, _ = kv.shape
    block = pl.BlockSpec((together * STRETCH, width), lambda c: (c, 0))
    return pl.pallas_call(
        functools.partial(attend_kernel, heads=heads),
        grid=(count // together,),
        in_specs=[
            block,
            block,
            pl.BlockSpec(
                (2, heads, tiles, neigh, together, TILE, HEAD_DIM), lambda c: (0, 0, 0, 0, c, 0, 0)
            ),
        ],
        out_specs=[block, block],
        out_shape=[jax.ShapeDtypeStruct(q.shape, BF16)] * 2,
        compiler_params=pltpu.CompilerParams(vmem_limit_bytes=VMEM),
        cost_estimate=pl.CostEstimate(
            flops=10 * rows * width * neigh * tiles * TILE, bytes_accessed=kv.size * 2, transcendentals=0
        ),
        name="attend",
    )(q, g, kv)


def split_kernel(core_ref, share_ref, own_ref, other_ref, *, rows):
    lane = lax.broadcasted_iota(jnp.int32, (share_ref.shape[0], 2 * rows), 1)
    first = core_ref[0] == 0
    for i in range(own_ref.shape[1] // (2 * rows)):
        even = share_ref[:, 4 * i * rows : (4 * i + 2) * rows].astype(F32)
        odd = share_ref[:, (4 * i + 2) * rows : (4 * i + 4) * rows].astype(F32)
        low = jnp.where(lane < rows, even, pltpu.roll(odd, rows, 1)).astype(BF16)
        high = jnp.where(lane < rows, pltpu.roll(even, rows, 1), odd).astype(BF16)
        own_ref[:, 2 * i * rows : 2 * (i + 1) * rows] = jnp.where(first, low, high)
        other_ref[:, 2 * i * rows : 2 * (i + 1) * rows] = jnp.where(first, high, low)


def split(core, share, rows):
    tokens, columns = share.shape
    whole = pl.BlockSpec((tokens, columns // 2), lambda: (0, 0))
    return pl.pallas_call(
        functools.partial(split_kernel, rows=rows),
        in_specs=[pl.BlockSpec(memory_space=pltpu.SMEM), pl.BlockSpec((tokens, columns), lambda: (0, 0))],
        out_specs=[whole] * 2,
        out_shape=[jax.ShapeDtypeStruct((tokens, columns // 2), BF16)] * 2,
        compiler_params=pltpu.CompilerParams(vmem_limit_bytes=16 << 20),
        cost_estimate=pl.CostEstimate(flops=0, bytes_accessed=4 << 20, transcendentals=0),
        name="split",
    )(core.reshape(1), share)


def step(array, axis, by):
    size = lax.axis_size(axis)
    return lax.ppermute(array, axis, [(i, (i + by) % size) for i in range(size)])


def local(inputs, w_query, cache_kv, nb_owner, nb_row, out_grad):
    nx, nz, nc = (lax.axis_size(a) for a in DP)
    ndp, nmp = nx * nz * nc, lax.axis_size("mp")
    mx, mz, mc = (lax.axis_index(a) for a in DP)
    my = lax.axis_index("mp")
    tokens, grad_rows = inputs[0], out_grad[0]
    length, d = tokens.shape
    width = w_query.shape[1]
    heads = width // HEAD_DIM
    db_rows, _, nb_len, _ = cache_kv.shape
    _, stretches, neigh = nb_owner.shape
    requests = stretches * neigh
    tiles = nb_len // TILE
    real = length - LEAD

    lanes = (0, HEAD_DIM - stretches)
    named = jnp.pad(nb_owner[0].T, ((0, TILE - neigh), lanes)) + jnp.pad(nb_row[0].T, ((neigh, TILE - 2 * neigh), lanes))
    message = cut(named.astype(BF16), cache_kv)
    held = lax.all_to_all(message, DP, split_axis=0, concat_axis=0, tiled=True)

    block = d // nmp
    fans = [lax.dynamic_slice(w_query, ((my + by) % nmp * block, 0), (block, width)) for by in range(nmp)]
    fans = [step(a, "mp", by) if by else a for by, a in enumerate(fans)]
    held, fans = lax.optimization_barrier((held, fans))

    named = held[:, db_rows, : 2 * neigh, :stretches].astype(jnp.int32)
    ids = named[:, :neigh] * (db_rows + 1) + named[:, neigh:]
    send = pick(ids.reshape(-1), held.reshape(-1, TILE, HEAD_DIM))
    got = lax.all_to_all(
        send.reshape(ndp, requests, TILE, HEAD_DIM), DP, split_axis=0, concat_axis=0, tiled=True
    )

    late, weights, grad_rows, _ = lax.optimization_barrier((tokens, w_query, grad_rows, held))
    block = d // nx
    share = [lax.dynamic_slice(late, (SKIP, (mx + by) % nx * block), (length - SKIP, block)) for by in range(nx)]
    share = [split(mc, step(a, "x", by) if by else a, d // ndp) for by, a in enumerate(share)]

    def shifted(array):
        return jnp.concatenate([array[LEAD:], jnp.zeros((LEAD, array.shape[1]), array.dtype)], 0)

    q = shifted(jnp.dot(late, weights, preferred_element_type=F32).astype(BF16))
    g = shifted(grad_rows)
    got, share, q, g = lax.optimization_barrier((got, share, q, g))

    out, dq = attend(q, g, got.reshape(2, heads, tiles, neigh, stretches, TILE, HEAD_DIM))
    dq = jnp.concatenate([jnp.zeros((LEAD - SKIP, width), BF16), dq[:real]], 0)

    groups = [step(dq, "mp", by) if by else dq for by in range(nmp)]
    mine = other = 0.0
    order = sorted(range(nx), key=lambda by: min(by, nx - by))
    for by in order:
        near = step(dq, "x", by) if by else dq
        if by == 1:
            own = lax.dot_general(dq, fans[0], BOTH_LAST, preferred_element_type=F32).astype(BF16)
            near, own = lax.optimization_barrier((near, own))
        if by == order[-1]:
            near, mine, groups[1], _ = lax.optimization_barrier((near, mine, groups[1], other))
        other += lax.dot_general(share[by][1], near, BOTH_FIRST, preferred_element_type=F32)
        mine += lax.dot_general(share[by][0], near, BOTH_FIRST, preferred_element_type=F32)
    mine += step(other, "core", 1)
    pairs = mine.reshape(nz // 2, 2, -1, width)
    away = lax.dynamic_index_in_dim(pairs, 1 - mz % 2, 1, keepdims=False)
    mine = lax.dynamic_index_in_dim(pairs, mz % 2, 1, keepdims=False)
    up = lax.ppermute(away[..., : width // 2], "z", [(i, i ^ 1) for i in range(nz)])
    down = lax.ppermute(away[..., width // 2 :], "z", [(i, ((i + 1) ^ 1) - 1) for i in range(1, nz - 1)] + [(0, nz - 1), (nz - 1, 0)])
    parts = [own, lax.dot_general(groups[1], fans[1], BOTH_LAST, preferred_element_type=F32).astype(BF16)]
    up, parts = lax.optimization_barrier((up, parts))
    mine += jnp.concatenate([up, down], -1)
    terms = [lax.dynamic_index_in_dim(mine, (mz // 2 + by) % (nz // 2), 0, keepdims=False) for by in range(nz // 2)]
    terms = [step(a, "z", 2 * by) if by else a for by, a in enumerate(terms)]
    for by in range(2, nmp):
        near, _ = lax.optimization_barrier((groups[by], mine if by < nmp - 1 else terms[1]))
        parts.append(lax.dot_general(near, fans[by], BOTH_LAST, preferred_element_type=F32).astype(BF16))
    query_grad = sum(terms)
    part = sum(a.astype(F32) for a in parts).astype(BF16)
    attended = jnp.concatenate([jnp.zeros((LEAD, width), BF16), out[:real]], 0)
    input_grad = jnp.concatenate([jnp.zeros((SKIP, d // nmp), BF16), part], 0)
    return attended[None], input_grad[None], query_grad


def solution(mesh):
    fine = Mesh(mesh.devices.reshape(4, 8, 2, 4), ("x", "z", "core", "mp"))
    return jax.shard_map(
        local,
        mesh=fine,
        in_specs=(
            P(DP, None, None),
            P(None, "mp"),
            P(DP, None, None, "mp"),
            P(DP, None, None),
            P(DP, None, None),
            P(DP, None, "mp"),
        ),
        out_specs=(P(DP, None, "mp"), P(DP, None, "mp"), P(DP, "mp")),
        check_vma=False,
    )
```

```python
import functools

import jax
import jax.numpy as jnp
from jax import lax
from jax.experimental import pallas as pl
from jax.experimental.pallas import tpu as pltpu
from jax.sharding import Mesh
from jax.sharding import PartitionSpec as P

HEAD_DIM = 128
STRETCH = 64
LEAD = STRETCH - 1
TILE = 16
SKIP = LEAD // TILE * TILE
DP = ("x", "z", "core")
VMEM = 32 << 20
BF16, F32 = jnp.bfloat16, jnp.float32
BOTH_LAST = (((1,), (1,)), ((), ()))
BOTH_FIRST = (((0,), (0,)), ((), ()))


def cut_kernel(named_ref, cache_ref, out_ref):
    rows = cache_ref.shape[0]
    _, heads, tiles, _, _, _ = out_ref.shape
    for head in range(heads):
        cols = slice(head * HEAD_DIM, (head + 1) * HEAD_DIM)
        for tile in range(tiles):
            out_ref[0, head, tile, :rows] = cache_ref[:, 0, tile * TILE : (tile + 1) * TILE, cols]
            out_ref[0, head, tile, rows] = named_ref[...]


def cut(named, cache):
    rows, _, nb_len, width = cache.shape
    tiles, heads = nb_len // TILE, width // HEAD_DIM
    return pl.pallas_call(
        cut_kernel,
        grid=(2,),
        in_specs=[
            pl.BlockSpec(named.shape, lambda a: (0, 0)),
            pl.BlockSpec((rows, 1, nb_len, width), lambda a: (0, a, 0, 0)),
        ],
        out_specs=pl.BlockSpec((1, heads, tiles, rows + 1, TILE, HEAD_DIM), lambda a: (a, 0, 0, 0, 0, 0)),
        out_shape=jax.ShapeDtypeStruct((2, heads, tiles, rows + 1, TILE, HEAD_DIM), BF16),
        compiler_params=pltpu.CompilerParams(vmem_limit_bytes=60 << 20),
        cost_estimate=pl.CostEstimate(flops=0, bytes_accessed=4 << 20, transcendentals=0),
        name="cut",
    )(named, cache).reshape(-1, rows + 1, TILE, HEAD_DIM)


def pick_kernel(ids_ref, tiles_ref, out_ref, *, slots):
    base = pl.program_id(0) * slots
    for slot in range(slots):
        out_ref[slot] = tiles_ref[ids_ref[base + slot]]


def pick(ids, tiles):
    count, slots = ids.shape[0], 128
    return pl.pallas_call(
        functools.partial(pick_kernel, slots=slots),
        grid_spec=pltpu.PrefetchScalarGridSpec(
            num_scalar_prefetch=1,
            grid=(count // slots,),
            in_specs=[pl.BlockSpec(tiles.shape, lambda s, ids: (0, 0, 0))],
            out_specs=pl.BlockSpec((slots,) + tiles.shape[1:], lambda s, ids: (s, 0, 0)),
        ),
        out_shape=jax.ShapeDtypeStruct((count,) + tiles.shape[1:], tiles.dtype),
        compiler_params=pltpu.CompilerParams(vmem_limit_bytes=VMEM),
        cost_estimate=pl.CostEstimate(flops=0, bytes_accessed=6 << 20, transcendentals=0),
        name="pick",
    )(ids, tiles)


def attend_kernel(q_ref, g_ref, kv_ref, out_ref, dq_ref, *, heads):
    for i in range(q_ref.shape[0] // STRETCH):
        rows = pl.ds(i * STRETCH, STRETCH)
        kv = kv_ref.at[:, :, :, :, i]
        attend_stretch(q_ref.at[rows], g_ref.at[rows], kv, out_ref.at[rows], dq_ref.at[rows], heads)


def attend_stretch(q_ref, g_ref, kv_ref, out_ref, dq_ref, heads):
    scale = HEAD_DIM ** (-0.5)
    cols = [slice(h * HEAD_DIM, (h + 1) * HEAD_DIM) for h in range(heads)]
    keys = [kv_ref[0, h].reshape(-1, HEAD_DIM) for h in range(heads)]
    values = [kv_ref[1, h].reshape(-1, HEAD_DIM) for h in range(heads)]
    scores = [
        lax.dot_general(q_ref[:, c], k, BOTH_LAST, preferred_element_type=F32)
        for c, k in zip(cols, keys)
    ]
    dprobs = [
        lax.dot_general(g_ref[:, c], v, BOTH_LAST, preferred_element_type=F32)
        for c, v in zip(cols, values)
    ]
    probs, dscores = [], []
    for score, dprob in zip(scores, dprobs):
        score = score * scale
        exps = jnp.exp(score - jnp.max(score, axis=-1, keepdims=True))
        prob = exps * (1.0 / jnp.sum(exps, axis=-1, keepdims=True))
        delta = jnp.sum(dprob * prob, axis=-1, keepdims=True)
        probs.append(prob.astype(BF16))
        dscores.append((prob * (dprob - delta) * scale).astype(BF16))
    for c, k, v, prob, dscore in zip(cols, keys, values, probs, dscores):
        out_ref[:, c] = jnp.dot(prob, v, preferred_element_type=F32).astype(BF16)
        dq_ref[:, c] = jnp.dot(dscore, k, preferred_element_type=F32).astype(BF16)


def attend(q, g, kv):
    rows, width = q.shape
    count, together = rows // STRETCH, 4
    _, heads, tiles, neigh, _, _, _ = kv.shape
    block = pl.BlockSpec((together * STRETCH, width), lambda c: (c, 0))
    return pl.pallas_call(
        functools.partial(attend_kernel, heads=heads),
        grid=(count // together,),
        in_specs=[
            block,
            block,
            pl.BlockSpec(
                (2, heads, tiles, neigh, together, TILE, HEAD_DIM), lambda c: (0, 0, 0, 0, c, 0, 0)
            ),
        ],
        out_specs=[block, block],
        out_shape=[jax.ShapeDtypeStruct(q.shape, BF16)] * 2,
        compiler_params=pltpu.CompilerParams(vmem_limit_bytes=VMEM),
        cost_estimate=pl.CostEstimate(
            flops=10 * rows * width * neigh * tiles * TILE, bytes_accessed=kv.size * 2, transcendentals=0
        ),
        name="attend",
    )(q, g, kv)


def split_kernel(core_ref, share_ref, own_ref, other_ref, *, rows):
    lane = lax.broadcasted_iota(jnp.int32, (share_ref.shape[0], 2 * rows), 1)
    first = core_ref[0] == 0
    for i in range(own_ref.shape[1] // (2 * rows)):
        even = share_ref[:, 4 * i * rows : (4 * i + 2) * rows].astype(F32)
        odd = share_ref[:, (4 * i + 2) * rows : (4 * i + 4) * rows].astype(F32)
        low = jnp.where(lane < rows, even, pltpu.roll(odd, rows, 1)).astype(BF16)
        high = jnp.where(lane < rows, pltpu.roll(even, rows, 1), odd).astype(BF16)
        own_ref[:, 2 * i * rows : 2 * (i + 1) * rows] = jnp.where(first, low, high)
        other_ref[:, 2 * i * rows : 2 * (i + 1) * rows] = jnp.where(first, high, low)


def split(core, share, rows):
    tokens, columns = share.shape
    whole = pl.BlockSpec((tokens, columns // 2), lambda: (0, 0))
    return pl.pallas_call(
        functools.partial(split_kernel, rows=rows),
        in_specs=[pl.BlockSpec(memory_space=pltpu.SMEM), pl.BlockSpec((tokens, columns), lambda: (0, 0))],
        out_specs=[whole] * 2,
        out_shape=[jax.ShapeDtypeStruct((tokens, columns // 2), BF16)] * 2,
        compiler_params=pltpu.CompilerParams(vmem_limit_bytes=16 << 20),
        cost_estimate=pl.CostEstimate(flops=0, bytes_accessed=4 << 20, transcendentals=0),
        name="split",
    )(core.reshape(1), share)


def step(array, axis, by):
    size = lax.axis_size(axis)
    return lax.ppermute(array, axis, [(i, (i + by) % size) for i in range(size)])


def local(inputs, w_query, cache_kv, nb_owner, nb_row, out_grad):
    nx, nz, nc = (lax.axis_size(a) for a in DP)
    ndp, nmp = nx * nz * nc, lax.axis_size("mp")
    mx, mz, mc = (lax.axis_index(a) for a in DP)
    my = lax.axis_index("mp")
    tokens, grad_rows = inputs[0], out_grad[0]
    length, d = tokens.shape
    width = w_query.shape[1]
    heads = width // HEAD_DIM
    db_rows, _, nb_len, _ = cache_kv.shape
    _, stretches, neigh = nb_owner.shape
    requests = stretches * neigh
    tiles = nb_len // TILE
    real = length - LEAD

    lanes = (0, HEAD_DIM - stretches)
    named = jnp.pad(nb_owner[0].T, ((0, TILE - neigh), lanes)) + jnp.pad(nb_row[0].T, ((neigh, TILE - 2 * neigh), lanes))
    message = cut(named.astype(BF16), cache_kv)
    held = lax.all_to_all(message, DP, split_axis=0, concat_axis=0, tiled=True)

    block = d // nmp
    fans = [lax.dynamic_slice(w_query, ((my + by) % nmp * block, 0), (block, width)) for by in range(nmp)]
    fans = [step(a, "mp", by) if by else a for by, a in enumerate(fans)]
    held, fans = lax.optimization_barrier((held, fans))

    named = held[:, db_rows, : 2 * neigh, :stretches].astype(jnp.int32)
    ids = named[:, :neigh] * (db_rows + 1) + named[:, neigh:]
    send = pick(ids.reshape(-1), held.reshape(-1, TILE, HEAD_DIM))
    got = lax.all_to_all(
        send.reshape(ndp, requests, TILE, HEAD_DIM), DP, split_axis=0, concat_axis=0, tiled=True
    )

    late, weights, grad_rows, _ = lax.optimization_barrier((tokens, w_query, grad_rows, held))
    block = d // nx
    share = [lax.dynamic_slice(late, (SKIP, (mx + by) % nx * block), (length - SKIP, block)) for by in range(nx)]
    share = [split(mc, step(a, "x", by) if by else a, d // ndp) for by, a in enumerate(share)]

    def shifted(array):
        return jnp.concatenate([array[LEAD:], jnp.zeros((LEAD, array.shape[1]), array.dtype)], 0)

    q = shifted(jnp.dot(late, weights, preferred_element_type=F32).astype(BF16))
    g = shifted(grad_rows)
    got, share, q, g = lax.optimization_barrier((got, share, q, g))

    out, dq = attend(q, g, got.reshape(2, heads, tiles, neigh, stretches, TILE, HEAD_DIM))
    dq = jnp.concatenate([jnp.zeros((LEAD - SKIP, width), BF16), dq[:real]], 0)

    groups = [step(dq, "mp", by) if by else dq for by in range(nmp)]
    mine = other = 0.0
    order = sorted(range(nx), key=lambda by: min(by, nx - by))
    for by in order:
        near = step(dq, "x", by) if by else dq
        if by == 1:
            own = lax.dot_general(dq, fans[0], BOTH_LAST, preferred_element_type=F32).astype(BF16)
            near, own = lax.optimization_barrier((near, own))
        if by == order[-1]:
            near, mine, groups[1], _ = lax.optimization_barrier((near, mine, groups[1], other))
        other += lax.dot_general(share[by][1], near, BOTH_FIRST, preferred_element_type=F32)
        mine += lax.dot_general(share[by][0], near, BOTH_FIRST, preferred_element_type=F32)
    mine += step(other, "core", 1)
    pairs = mine.reshape(nz // 2, 2, -1, width)
    away = lax.dynamic_index_in_dim(pairs, 1 - mz % 2, 1, keepdims=False)
    mine = lax.dynamic_index_in_dim(pairs, mz % 2, 1, keepdims=False)
    up = lax.ppermute(away[..., : width // 2], "z", [(i, i ^ 1) for i in range(nz)])
    down = lax.ppermute(away[..., width // 2 :], "z", [(i, ((i + 1) ^ 1) - 1) for i in range(1, nz - 1)] + [(0, nz - 1), (nz - 1, 0)])
    parts = [own, lax.dot_general(groups[1], fans[1], BOTH_LAST, preferred_element_type=F32).astype(BF16)]
    up, parts = lax.optimization_barrier((up, parts))
    mine += jnp.concatenate([up, down], -1)
    terms = [lax.dynamic_index_in_dim(mine, (mz // 2 + by) % (nz // 2), 0, keepdims=False) for by in range(nz // 2)]
    terms = [step(a, "z", 2 * by) if by else a for by, a in enumerate(terms)]
    for by in range(2, nmp):
        near, _ = lax.optimization_barrier((groups[by], mine if by < nmp - 1 else terms[1]))
        parts.append(lax.dot_general(near, fans[by], BOTH_LAST, preferred_element_type=F32).astype(BF16))
    query_grad = sum(terms)
    part = sum(a.astype(F32) for a in parts).astype(BF16)
    attended = jnp.concatenate([jnp.zeros((LEAD, width), BF16), out[:real]], 0)
    input_grad = jnp.concatenate([jnp.zeros((SKIP, d // nmp), BF16), part], 0)
    return attended[None], input_grad[None], query_grad


def solution(mesh):
    fine = Mesh(mesh.devices.reshape(4, 8, 2, 4), ("x", "z", "core", "mp"))
    return jax.shard_map(
        local,
        mesh=fine,
        in_specs=(
            P(DP, None, None),
            P(None, "mp"),
            P(DP, None, None, "mp"),
            P(DP, None, None),
            P(DP, None, None),
            P(DP, None, "mp"),
        ),
        out_specs=(P(DP, None, "mp"), P(DP, None, "mp"), P(DP, "mp")),
        check_vma=False,
    )
```
